256 devices in a mesh: dp: 64 (over z, x_lo, y), tensor: 4 (over x_hi, core).
Axes of the slice: x: 4 (x_hi: 2, x_lo: 2; x = x_hi * 2 + x_lo), y: 4, z: 8, core: 2. Of those that a mesh axis runs over, the one named last changes fastest.
Arguments:
- head_outputs: bfloat16 [32768, 4096], P('dp', 'tensor'), may hold values from -6 to 6
- output_gradient: bfloat16 [32768, 4608], P(('dp', 'tensor')), may hold values from -6 to 6
- frozen_weight: bfloat16 [4608, 4096], P('dp', 'tensor'), may hold values from -0.09375 to 0.09375
- adapter_down_factors: bfloat16 [4096, 8192], P('tensor', 'dp'), may hold values from -0.09375 to 0.09375
- adapter_up_factors: bfloat16 [8192, 4608], P('dp'), may hold values from -0.09375 to 0.09375
- tenant_index: int32 [32768], P('dp'), may hold values from 0 to 511, as said below
- tenant_group_counts: int32 [64], P('dp'), may hold values from 32 to 512, as said below
Outputs:
- head_feature_gradient: bfloat16 [32768, 4096], P('dp', 'tensor')
- down_factor_gradient: float32 [4096, 8192], P('tensor', 'dp')
- up_factor_gradient: float32 [8192, 4608], P('dp')
The draws below stay inside these ranges and needn't reach their ends.
Inputs may be any that keep to these rules, and one draw needn't show every extreme that they name: `tenant_index`: the tenants of group g (rows g * 512 to (g + 1) * 512 - 1) are g * 8 to (g + 1) * 8 - 1. `tenant_group_counts`: some group holds exactly 512 live rows.
All inputs are finite; a program needn't handle non-finite values.
Results may differ from the reference program's by a relative error of at most 0.0034.
Values may be sent and summed in bfloat16 or wider, within the bound.
No kernel may reach another device: no remote copies, remote signals or barrier semaphores. Data moves between devices by JAX's collectives and lax.ppermute only.
A program may use at most 128 MiB of HBM per device.

```python
import jax
import jax.numpy as jnp
from jax import lax

MODEL_WIDTH = 4608
HEAD_FEATURES = 4096
ADAPTER_RANK = 16
TEN_DEV = 8
TENANT_COUNT = 512
CAP = 512
ROWS = 32768
N_DP = 64


def draw_tenant_index(key, part):
    key = jax.random.fold_in(key, 7)
    group_of = jnp.arange(CAP * N_DP, dtype=jnp.int32) // CAP
    inside = jax.random.randint(key, (CAP * N_DP,), 0, TEN_DEV)
    return (group_of * TEN_DEV + inside).astype(jnp.int32)


def draw_tenant_group_counts(key, part):
    key = jax.random.fold_in(key, 11)
    first, second, third = jax.random.split(key, 3)
    light = jax.random.randint(first, (N_DP,), CAP // 16, CAP // 2)
    heavy = jax.random.randint(second, (N_DP,), CAP // 2, CAP + 1)
    order = jax.random.permutation(third, N_DP)
    ranking = jnp.zeros((N_DP,), jnp.int32).at[order].set(jnp.arange(N_DP, dtype=jnp.int32))
    counts = jnp.where(ranking < max(N_DP // 8, 1), heavy, light)
    return jnp.where(ranking == 0, CAP, counts).astype(jnp.int32)


def block_scale(rng, shape, shards, low, high):
    gain = 1.0
    for dim, blocks in shards:
        steps = jax.random.uniform(jax.random.fold_in(jax.random.fold_in(rng, 6), dim), (blocks,), jnp.float32, low / len(shards), high / len(shards))
        gain = gain * jnp.repeat(jnp.exp(steps), shape[dim] // blocks).reshape((-1,) + (1,) * (len(shape) - 1 - dim))
    return gain


def bell_draw(own_key, dims, deviation, most, pieces=(), held_as=jnp.bfloat16):
    gain = block_scale(own_key, dims, pieces, -0.22, 0.18) if pieces else 1.0
    array = jax.random.normal(own_key, dims, jnp.float32) * deviation * gain
    return jnp.minimum(jnp.maximum(array, -most), most).astype(held_as)


def setup_inputs(seed: int = 0) -> dict:
    arg_keys = jax.random.split(jax.random.key(seed), 8)
    return {
        "head_outputs": bell_draw(arg_keys[0], (ROWS, HEAD_FEATURES), 1.0, 6.0, ((0, 64), (1, 4))),
        "output_gradient": bell_draw(arg_keys[1], (ROWS, MODEL_WIDTH), 1.0, 6.0, ((0, 256),)),
        "frozen_weight": bell_draw(arg_keys[2], (MODEL_WIDTH, HEAD_FEATURES), MODEL_WIDTH ** -0.5, 0.09375, ((0, 64), (1, 4))),
        "adapter_down_factors": bell_draw(arg_keys[3], (HEAD_FEATURES, TENANT_COUNT * ADAPTER_RANK), HEAD_FEATURES ** -0.5, 0.09375, ((0, 4), (1, 64))),
        "adapter_up_factors": bell_draw(arg_keys[4], (TENANT_COUNT * ADAPTER_RANK, MODEL_WIDTH), MODEL_WIDTH ** -0.5, 0.09375, ((0, 64),)),
        "tenant_index": draw_tenant_index(jax.random.fold_in(arg_keys[7], 71), 0),
        "tenant_group_counts": draw_tenant_group_counts(jax.random.fold_in(arg_keys[7], 71), 0),
    }


ADAPTER_SCALE = 2.0


def group_grads(head_outputs, output_gradient, down_factor_block, up_block, tenant_index, count, frozen_weight):
    position = jnp.arange(head_outputs.shape[0], dtype=jnp.int32)
    active_rows = position < count
    slot_lookup = jnp.arange(down_factor_block.shape[1], dtype=jnp.int32) // ADAPTER_RANK
    select_rows = (active_rows[:, None] & (slot_lookup[None, :] == (tenant_index % TEN_DEV)[:, None])).astype(jnp.float32)
    adapter_input = (jnp.dot(head_outputs, down_factor_block, preferred_element_type=jnp.float32) * select_rows).astype(jnp.bfloat16)
    adapter_backward = (jnp.dot(output_gradient, up_block.T, preferred_element_type=jnp.float32) * select_rows).astype(jnp.bfloat16)
    frozen_term = jnp.dot(output_gradient, frozen_weight, preferred_element_type=jnp.float32)
    adapter_term = jnp.dot(adapter_backward, down_factor_block.T, preferred_element_type=jnp.float32)
    head_feature_gradient = (active_rows[:, None].astype(jnp.float32) * frozen_term + ADAPTER_SCALE * adapter_term).astype(jnp.bfloat16)
    down_factor_gradient = ADAPTER_SCALE * jnp.dot(head_outputs.T, adapter_backward, preferred_element_type=jnp.float32)
    up_factor_gradient = ADAPTER_SCALE * jnp.dot(adapter_input.T, output_gradient, preferred_element_type=jnp.float32)
    return head_feature_gradient, down_factor_gradient, up_factor_gradient


def reference(head_outputs, output_gradient, frozen_weight, adapter_down_factors, adapter_up_factors, tenant_index, tenant_group_counts):
    feature_span = TEN_DEV * ADAPTER_RANK
    acts_g = head_outputs.reshape(N_DP, CAP, HEAD_FEATURES)
    grad_g = output_gradient.reshape(N_DP, CAP, MODEL_WIDTH)
    down_gradient_group = jnp.transpose(adapter_down_factors.reshape(HEAD_FEATURES, N_DP, feature_span), (1, 0, 2))
    up_gradient_group = adapter_up_factors.reshape(N_DP, feature_span, MODEL_WIDTH)
    ids_g = tenant_index.reshape(N_DP, CAP)

    def one_group(items):
        return group_grads(items[0], items[1], items[2], items[3], items[4], items[5], frozen_weight)

    head_feature_gradient, down_factor_gradient, up_factor_gradient = lax.map(one_group, (acts_g, grad_g, down_gradient_group, up_gradient_group, ids_g, tenant_group_counts))
    head_feature_gradient = head_feature_gradient.reshape(ROWS, HEAD_FEATURES)
    down_factor_gradient = jnp.transpose(down_factor_gradient, (1, 0, 2)).reshape(HEAD_FEATURES, N_DP * feature_span)
    up_factor_gradient = up_factor_gradient.reshape(N_DP * feature_span, MODEL_WIDTH)
    return head_feature_gradient, down_factor_gradient, up_factor_gradient
```

```python
import jax
import jax.numpy as jnp
from jax import lax
from jax.experimental import pallas as pl
from jax.experimental.pallas import tpu as pltpu
from jax.sharding import PartitionSpec as P

ADAPTER_RANK = 16
TEN_DEV = 8
ADAPTER_SCALE = 2.0
NZ, NX, NY = 8, 2, 4


def contract(left, right, left_dim, right_dim):
    return lax.dot_general(
        left, right, (((left_dim,), (right_dim,)), ((), ())), preferred_element_type=jnp.float32
    )


def fetch(x, dz=0, dx=0, dy=0):
    pairs = []
    for z in range(NZ):
        for a in range(NX):
            for y in range(NY):
                source = (((z + dz) % NZ) * NX + (a + dx) % NX) * NY + (y + dy) % NY
                pairs.append((source, (z * NX + a) * NY + y))
    return lax.ppermute(x, "dp", pairs)


def swap_tensor(x, mask):
    return lax.ppermute(x, "tensor", [(t, t ^ mask) for t in range(4)])


def split_kernel(start_ref, g_ref, out_ref):
    width = out_ref.shape[2]
    for block in range(NZ):
        slot = lax.rem(block - start_ref[0] + NZ, NZ)
        out_ref[slot] = g_ref[:, block * width : (block + 1) * width]


def split_columns(gradients, start):
    rows, depth = gradients.shape
    step = rows // 4
    width = depth // NZ
    return pl.pallas_call(
        split_kernel,
        grid_spec=pltpu.PrefetchScalarGridSpec(
            num_scalar_prefetch=1,
            grid=(4,),
            in_specs=[pl.BlockSpec((step, depth), lambda i, s: (i, 0))],
            out_specs=pl.BlockSpec((NZ, step, width), lambda i, s: (0, i, 0)),
        ),
        out_shape=jax.ShapeDtypeStruct((NZ, rows, width), gradients.dtype),
        compiler_params=pltpu.CompilerParams(vmem_limit_bytes=32 * 1024 * 1024),
    )(start, gradients)


def in_y_order(chunks, y):
    one = chunks[0]
    shape = one.shape[:-2] + (NY,) + one.shape[-2:]
    buffer = jnp.zeros(shape, one.dtype)
    axis = len(shape) - 3
    for offset, chunk in chunks.items():
        buffer = lax.dynamic_update_slice_in_dim(
            buffer, jnp.expand_dims(chunk, axis), (y + offset) % NY, axis
        )
    return buffer


def body(
    head_outputs,
    output_gradient,
    frozen_weight,
    adapter_down_factors,
    adapter_up_factors,
    tenant_index,
    tenant_group_counts,
):
    row_count = head_outputs.shape[0]
    part_rows, depth = output_gradient.shape
    shard_rows, feature_width = frozen_weight.shape
    a_width = feature_width * 9 // 16
    group = lax.axis_index("dp")
    z, xl, y = group // (NX * NY), (group // NY) % NX, group % NY
    tensor = lax.axis_index("tensor")

    other = fetch(frozen_weight, dx=1)
    pair = jnp.where(xl == 0, jnp.stack([frozen_weight, other]), jnp.stack([other, frozen_weight]))
    pair_a, pair_b = pair[:, :, :a_width], pair[:, :, a_width:]

    from_core = swap_tensor(output_gradient, 1)
    from_chip = swap_tensor(output_gradient, 2)
    from_both = swap_tensor(from_chip, 1)

    b_p = fetch(pair_b, dy=1)
    b_m = fetch(pair_b, dy=-1)
    b_o = jnp.stack([fetch(b_p[0], dy=1), fetch(b_m[1], dy=-1)])
    b_own = in_y_order({0: pair_b, 1: b_p, 3: b_m, 2: b_o}, y)
    b_own = b_own.reshape(NX * NY * shard_rows, -1)

    a_p1, a_m1 = fetch(pair_a, dz=1), fetch(pair_a, dz=-1)
    a_p2, a_m2 = fetch(a_p1, dz=1), fetch(a_m1, dz=-1)
    first = jnp.stack([a_m1, pair_a, a_p1, a_p2])
    a_p3, a_m3 = fetch(a_p2, dz=1), fetch(a_m2, dz=-1)
    a_o = fetch(a_p3, dz=1)
    second = jnp.stack([a_p3, a_o, a_m3, a_m2])

    b_p1, b_m1 = fetch(b_own, dz=1), fetch(b_own, dz=-1)
    b_p2, b_m2 = fetch(b_p1, dz=1), fetch(b_m1, dz=-1)
    b_p3, b_m3 = fetch(b_p2, dz=1), fetch(b_m2, dz=-1)
    cut = b_own.shape[0] // 3 // 8 * 8
    b_o = jnp.concatenate([fetch(b_p3[:cut], dz=1), fetch(b_m3[cut:], dz=-1)], 0)

    f_p, f_m = fetch(first, dy=1), fetch(first, dy=-1)
    f_o = fetch(f_m, dy=-1)
    s_p, s_m = fetch(second, dy=1), fetch(second, dy=-1)
    s_o = fetch(s_p, dy=1)
    first_all = in_y_order({0: first, 1: f_p, 3: f_m, 2: f_o}, y)
    second_all = in_y_order({0: second, 1: s_p, 3: s_m, 2: s_o}, y)

    gradients = jnp.zeros((row_count, depth), output_gradient.dtype)
    for block, place in (
        (output_gradient, tensor),
        (from_core, tensor ^ 1),
        (from_chip, tensor ^ 2),
        (from_both, tensor ^ 3),
    ):
        gradients = lax.dynamic_update_slice_in_dim(gradients, block, place * part_rows, 0)
    by_z = split_columns(gradients, ((z + NZ - 1) % NZ).reshape(1))

    adapter_width = adapter_down_factors.shape[1]
    partial = jnp.dot(head_outputs, adapter_down_factors, preferred_element_type=jnp.float32)
    chip_sum = partial + swap_tensor(partial, 1)
    summed = chip_sum + swap_tensor(chip_sum, 2)
    position = jnp.arange(row_count, dtype=jnp.int32)
    active_rows = position < tenant_group_counts[0]
    slot_lookup = jnp.arange(adapter_width, dtype=jnp.int32) // ADAPTER_RANK
    select_rows = (
        active_rows[:, None] & (slot_lookup[None, :] == (tenant_index % TEN_DEV)[:, None])
    ).astype(jnp.float32)
    adapter_input = (summed * select_rows).astype(jnp.bfloat16)
    adapter_backward = (contract(gradients, adapter_up_factors, 1, 1) * select_rows).astype(
        jnp.bfloat16
    )
    down_factor_gradient = ADAPTER_SCALE * contract(head_outputs, adapter_backward, 0, 0)
    up_factor_gradient = ADAPTER_SCALE * contract(adapter_input, gradients, 0, 0)
    adapter_term = contract(adapter_backward, adapter_down_factors, 1, 1)

    b_chunks = (b_m1, b_own, b_p1, b_p2, b_p3, b_o, b_m3, b_m2)
    a_chunks = [first_all[i] for i in range(4)] + [second_all[i] for i in range(4)]
    live = active_rows[:, None].astype(jnp.float32)

    def product(chunks, order):
        total = None
        for i in order:
            term = contract(by_z[i], chunks[i].reshape(by_z.shape[2], -1), 1, 0)
            total = term if total is None else total + term
        return total

    a_total = product(a_chunks, range(8))
    b_total = product(b_chunks, (1, 0, 2, 3, 7, 4, 6, 5))
    head_feature_gradient = jnp.concatenate(
        [
            (live * a_total + ADAPTER_SCALE * adapter_term[:, :a_width]).astype(jnp.bfloat16),
            (live * b_total + ADAPTER_SCALE * adapter_term[:, a_width:]).astype(jnp.bfloat16),
        ],
        1,
    )
    return (head_feature_gradient, down_factor_gradient, up_factor_gradient)


def solution(mesh):
    in_specs = (
        P("dp", "tensor"),
        P(("dp", "tensor"), None),
        P("dp", "tensor"),
        P("tensor", "dp"),
        P("dp", None),
        P("dp"),
        P("dp"),
    )
    out_specs = (P("dp", "tensor"), P("tensor", "dp"), P("dp", None))
    return jax.shard_map(body, mesh=mesh, in_specs=in_specs, out_specs=out_specs, check_vma=False)
```

```python
import jax
import jax.numpy as jnp
from jax import lax
from jax.experimental import pallas as pl
from jax.experimental.pallas import tpu as pltpu
from jax.sharding import PartitionSpec as P

ADAPTER_RANK = 16
TEN_DEV = 8
ADAPTER_SCALE = 2.0
NZ, NX, NY = 8, 2, 4
Z_SETS = ((-1, 0, 1), (-2, 2), (-3, 3), (4,))


def contract(left, right, left_dim, right_dim):
    return lax.dot_general(
        left, right, (((left_dim,), (right_dim,)), ((), ())), preferred_element_type=jnp.float32
    )


def fetch(x, dz=0, dx=0, dy=0):
    pairs = []
    for z in range(NZ):
        for a in range(NX):
            for y in range(NY):
                source = (((z + dz) % NZ) * NX + (a + dx) % NX) * NY + (y + dy) % NY
                pairs.append((source, (z * NX + a) * NY + y))
    return lax.ppermute(x, "dp", pairs)


def swap_tensor(x, mask):
    return lax.ppermute(x, "tensor", [(t, t ^ mask) for t in range(4)])


def after(values, *others):
    out = lax.optimization_barrier(tuple(values) + tuple(others))
    return out[: len(values)]


def split_kernel(count, place_ref, g_ref, *refs):
    full_ref, *set_refs, b_ref, pieces = refs[count:]
    z, x, y = place_ref[1], place_ref[2], place_ref[3]
    width = b_ref.shape[2] // (NX * NY)
    full_ref[...] = g_ref[...]
    for p in range(NZ * NX * NY):
        pieces[p, :, :width] = g_ref[:, p * width : (p + 1) * width]

    def piece(dz, dx, dy):
        index = (lax.rem(z + (dz + NZ), NZ) * NX + lax.rem(x + dx, NX)) * NY + lax.rem(y + dy, NY)
        return pieces[index, :, :width]

    for ref, offsets in zip(set_refs, Z_SETS):
        for dy in range(NY):
            at = 0
            for dz in offsets:
                for dx in range(NX):
                    ref[dy, :, at : at + width] = piece(dz, dx, dy)
                    at += width
    for dz in range(NZ):
        at = 0
        for dy in range(NY):
            for dx in range(NX):
                b_ref[dz, :, at : at + width] = piece(dz, dx, dy)
                at += width


def split_columns(block, place, rows, held):
    step, depth = block.shape
    width = depth // (NZ * NX * NY)
    shapes = [(rows, depth)]
    shapes += [(NY, rows, len(o) * NX * width) for o in Z_SETS]
    shapes += [(NZ, rows, NX * NY * width)]
    specs = [pl.BlockSpec((step, depth), lambda i, s: (s[0], 0))]
    specs += [pl.BlockSpec((s[0], step, s[2]), lambda i, s: (0, s[0], 0)) for s in shapes[1:]]
    count = len(held)
    return pl.pallas_call(
        lambda place_ref, g_ref, *refs: split_kernel(count, place_ref, g_ref, *refs),
        grid_spec=pltpu.PrefetchScalarGridSpec(
            num_scalar_prefetch=1,
            grid=(1,),
            in_specs=[pl.BlockSpec((step, depth), lambda i, s: (0, 0))]
            + [pl.BlockSpec(memory_space=pl.ANY)] * count,
            out_specs=specs,
            scratch_shapes=[pltpu.VMEM((NZ * NX * NY, step, 128), block.dtype)],
        ),
        out_shape=[jax.ShapeDtypeStruct(s, block.dtype) for s in shapes],
        input_output_aliases={2 + i: i for i in range(count)},
        compiler_params=pltpu.CompilerParams(vmem_limit_bytes=40 * 1024 * 1024),
    )(place, block, *held)


def body(
    head_outputs,
    output_gradient,
    frozen_weight,
    adapter_down_factors,
    adapter_up_factors,
    tenant_index,
    tenant_group_counts,
):
    row_count = head_outputs.shape[0]
    feature_width = frozen_weight.shape[1]
    a_width = feature_width * 5 // 8
    group = lax.axis_index("dp")
    z, xl, y = group // (NX * NY), (group // NY) % NX, group % NY
    tensor = lax.axis_index("tensor")

    def place(mask):
        return jnp.stack([tensor ^ mask, z, xl, y]).astype(jnp.int32)

    other = fetch(frozen_weight, dx=1)
    from_core = swap_tensor(output_gradient, 1)
    partial = jnp.dot(head_outputs, adapter_down_factors, preferred_element_type=jnp.float32)
    from_core_partial = swap_tensor(partial, 1)
    split = split_columns(output_gradient, place(0), row_count, ())

    pa = jnp.concatenate([frozen_weight[:, :a_width], other[:, :a_width]], 0)
    pb = jnp.concatenate([frozen_weight[:, a_width:], other[:, a_width:]], 0)

    a_p1, a_m1 = fetch(pa, dz=1), fetch(pa, dz=-1)
    b_p, b_m, b_o = fetch(pb, dy=1), fetch(pb, dy=-1), fetch(pb, dy=2)
    (gradient_later,) = after([output_gradient], pa)
    from_chip = swap_tensor(gradient_later, 2)

    a_p1, a_m1, pa2 = after([a_p1, a_m1, pa])
    a_p2, a_m2 = fetch(a_p1, dz=1), fetch(a_m1, dz=-1)
    c1 = jnp.concatenate([a_m1, pa2, a_p1], 0)
    f1_p, f1_m = fetch(c1, dy=1), fetch(c1, dy=-1)
    (from_core,) = after([from_core], a_p1)
    split = split_columns(from_core, place(1), row_count, split)

    pb2, b_p, b_m, b_o = after([pb, b_p, b_m, b_o], c1)
    bq = jnp.concatenate([pb2, b_p, b_o, b_m], 0)
    b_p1, b_m1 = fetch(bq, dz=1), fetch(bq, dz=-1)

    a_p2, a_m2 = after([a_p2, a_m2], bq)
    a_p3, a_m3 = fetch(a_p2, dz=1), fetch(a_m2, dz=-1)
    c2 = jnp.concatenate([a_m2, a_p2], 0)
    f2_p, f2_m = fetch(c2, dy=1), fetch(c2, dy=-1)
    partial2, from_core_partial = after([partial, from_core_partial], c2)
    chip_sum = partial2 + from_core_partial
    from_chip_sum = swap_tensor(chip_sum, 2)

    f1_p, f1_m = after([f1_p, f1_m], c2)
    f1_o = fetch(f1_p, dy=1)
    a_p3, a_m3 = after([a_p3, a_m3], f1_p)
    a_4 = fetch(a_p3, dz=1)
    c3 = jnp.concatenate([a_m3, a_p3], 0)
    f3_p, f3_m = fetch(c3, dy=1), fetch(c3, dy=-1)

    b_p1, b_m1 = after([b_p1, b_m1], c3)
    b_p2, b_m2 = fetch(b_p1, dz=1), fetch(b_m1, dz=-1)
    (from_chip,) = after([from_chip], b_p1)
    from_both = swap_tensor(from_chip, 1)
    split = split_columns(from_chip, place(2), row_count, split)

    f2_p, f2_m, a_4 = after([f2_p, f2_m, a_4], b_p1)
    f2_o = fetch(f2_m, dy=-1)
    f4_p, f4_m = fetch(a_4, dy=1), fetch(a_4, dy=-1)
    (from_both,) = after([from_both], a_4)
    split = split_columns(from_both, place(3), row_count, split)

    f3_p, f3_m = after([f3_p, f3_m], a_4)
    f3_o = fetch(f3_m, dy=-1)

    b_p2, b_m2 = after([b_p2, b_m2], f3_p)
    b_p3, b_m3 = fetch(b_p2, dz=1), fetch(b_m2, dz=-1)

    f4_p, f4_m = after([f4_p, f4_m], b_p2)
    f4_o = fetch(f4_p, dy=1)

    b_p3, b_m3 = after([b_p3, b_m3], f4_p)
    cut = bq.shape[0] // 3 // 16 * 16
    b_4 = [fetch(b_p3[:cut], dz=1), fetch(b_m3[cut:], dz=-1)]

    gradients, *by_set, by_z = split
    adapter_width = adapter_down_factors.shape[1]
    summed = chip_sum + from_chip_sum
    position = jnp.arange(row_count, dtype=jnp.int32)
    active_rows = position < tenant_group_counts[0]
    slot_lookup = jnp.arange(adapter_width, dtype=jnp.int32) // ADAPTER_RANK
    select_rows = (
        active_rows[:, None] & (slot_lookup[None, :] == (tenant_index % TEN_DEV)[:, None])
    ).astype(jnp.float32)
    adapter_input = (summed * select_rows).astype(jnp.bfloat16)
    adapter_backward = (contract(gradients, adapter_up_factors, 1, 1) * select_rows).astype(
        jnp.bfloat16
    )
    down_factor_gradient = ADAPTER_SCALE * contract(head_outputs, adapter_backward, 0, 0)
    up_factor_gradient = ADAPTER_SCALE * contract(adapter_input, gradients, 0, 0)
    adapter_term = contract(adapter_backward, adapter_down_factors, 1, 1)

    def product(terms):
        total = None
        for left, right in terms:
            term = contract(left, right, 1, 0)
            total = term if total is None else total + term
        return total

    g1, g2, g3, g4 = by_set
    a_total = product(
        [
            (g1[0], c1),
            (g1[1], f1_p),
            (g1[3], f1_m),
            (g2[0], c2),
            (g1[2], f1_o),
            (g2[1], f2_p),
            (g2[3], f2_m),
            (g3[0], c3),
            (g4[0], a_4),
            (g3[1], f3_p),
            (g3[3], f3_m),
            (g2[2], f2_o),
            (g4[1], f4_p),
            (g4[3], f4_m),
            (g3[2], f3_o),
            (g4[2], f4_o),
        ]
    )
    b_total = product(
        [
            (by_z[0], bq),
            (by_z[1], b_p1),
            (by_z[7], b_m1),
            (by_z[2], b_p2),
            (by_z[6], b_m2),
            (by_z[3], b_p3),
            (by_z[5], b_m3),
            (by_z[4], jnp.concatenate(b_4, 0)),
        ]
    )
    live = active_rows[:, None].astype(jnp.float32)
    head_feature_gradient = jnp.concatenate(
        [
            (live * a_total + ADAPTER_SCALE * adapter_term[:, :a_width]).astype(jnp.bfloat16),
            (live * b_total + ADAPTER_SCALE * adapter_term[:, a_width:]).astype(jnp.bfloat16),
        ],
        1,
    )
    return (head_feature_gradient, down_factor_gradient, up_factor_gradient)


def solution(mesh):
    in_specs = (
        P("dp", "tensor"),
        P(("dp", "tensor"), None),
        P("dp", "tensor"),
        P("tensor", "dp"),
        P("dp", None),
        P("dp"),
        P("dp"),
    )
    out_specs = (P("dp", "tensor"), P("tensor", "dp"), P("dp", None))
    return jax.shard_map(body, mesh=mesh, in_specs=in_specs, out_specs=out_specs, check_vma=False)
```

```python
import jax
import jax.numpy as jnp
from jax import lax
from jax.experimental import pallas as pl
from jax.experimental.pallas import tpu as pltpu
from jax.sharding import PartitionSpec as P

ADAPTER_RANK = 16
TEN_DEV = 8
ADAPTER_SCALE = 2.0
NZ, NX, NY = 8, 2, 4


def contract(left, right, left_dim, right_dim):
    return lax.dot_general(
        left, right, (((left_dim,), (right_dim,)), ((), ())), preferred_element_type=jnp.float32
    )


def fetch(x, dz=0, dx=0, dy=0):
    pairs = []
    for z in range(NZ):
        for a in range(NX):
            for y in range(NY):
                source = (((z + dz) % NZ) * NX + (a + dx) % NX) * NY + (y + dy) % NY
                pairs.append((source, (z * NX + a) * NY + y))
    return lax.ppermute(x, "dp", pairs)


def swap_tensor(x, mask):
    return lax.ppermute(x, "tensor", [(t, t ^ mask) for t in range(4)])


def together(*values):
    return lax.optimization_barrier(values)


def split_kernel(count, place_ref, g_ref, *refs):
    full_ref, z_ref = refs[count:]
    width = z_ref.shape[2]
    full_ref[...] = g_ref[...]
    for block in range(NZ):
        slot = lax.rem(block - place_ref[1] + NZ, NZ)
        z_ref[slot] = g_ref[:, block * width : (block + 1) * width]


def split_columns(block, place, rows, held):
    step, depth = block.shape
    width = depth // NZ
    count = len(held)
    return pl.pallas_call(
        lambda place_ref, g_ref, *refs: split_kernel(count, place_ref, g_ref, *refs),
        grid_spec=pltpu.PrefetchScalarGridSpec(
            num_scalar_prefetch=1,
            grid=(1,),
            in_specs=[pl.BlockSpec((step, depth), lambda i, s: (0, 0))]
            + [pl.BlockSpec(memory_space=pl.ANY)] * count,
            out_specs=[
                pl.BlockSpec((step, depth), lambda i, s: (s[0], 0)),
                pl.BlockSpec((NZ, step, width), lambda i, s: (0, s[0], 0)),
            ],
        ),
        out_shape=[
            jax.ShapeDtypeStruct((rows, depth), block.dtype),
            jax.ShapeDtypeStruct((NZ, rows, width), block.dtype),
        ],
        input_output_aliases={2 + i: i for i in range(count)},
        compiler_params=pltpu.CompilerParams(vmem_limit_bytes=32 * 1024 * 1024),
    )(place, block, *held)


def put(buffer, chunk, index):
    return lax.dynamic_update_slice_in_dim(buffer, chunk[:, :, None], index % NY, 2)


def put_half(buffer, chunk, index, half):
    zero = jnp.int32(0)
    at = (zero, jnp.int32(half), (index % NY).astype(jnp.int32), zero, zero)
    return lax.dynamic_update_slice(buffer, chunk[:, None, None], at)


def body(
    head_outputs,
    output_gradient,
    frozen_weight,
    adapter_down_factors,
    adapter_up_factors,
    tenant_index,
    tenant_group_counts,
):
    row_count = head_outputs.shape[0]
    shard_rows, feature_width = frozen_weight.shape
    a_width = feature_width * 5 // 8
    b_width = feature_width - a_width
    group = lax.axis_index("dp").astype(jnp.int32)
    z, xl, y = group // (NX * NY), (group // NY) % NX, group % NY
    tensor = lax.axis_index("tensor").astype(jnp.int32)

    def place(mask):
        return jnp.stack([tensor ^ mask, z])

    def start_buffer(own):
        n = own.shape[0]
        return jnp.broadcast_to(own[:, :, None], (n, NX, NY, shard_rows, a_width))

    def flat(parts):
        return jnp.concatenate([p.reshape(-1, a_width) for p in parts], 0)

    def unflat(block, halves, wholes):
        cut = halves * shard_rows
        half = block[:cut].reshape(halves, shard_rows, a_width)
        return half, block[cut:].reshape(wholes, NX, shard_rows, a_width)

    def product(start, terms):
        total = start
        for left, right in terms:
            term = contract(left, right.reshape(left.shape[1], -1), 1, 0)
            total = term if total is None else total + term
        return total

    own_a, own_b = frozen_weight[:, :a_width], frozen_weight[:, a_width:]
    other = fetch(frozen_weight, dx=1)
    y_b = [fetch(own_b, dy=1), fetch(own_b, dy=-1), fetch(own_b, dy=2)]
    from_core = swap_tensor(output_gradient, 1)
    partial = jnp.dot(head_outputs, adapter_down_factors, preferred_element_type=jnp.float32)
    split = split_columns(output_gradient, place(0), row_count, ())

    other, from_core, partial, gradient_later, *rest = together(
        other, from_core, partial, output_gradient, *y_b, *split
    )
    y_b, split = rest[:3], rest[3:]
    far_a, far_b = other[:, :a_width], other[:, a_width:]
    pa = jnp.where(xl == 0, jnp.stack([own_a, far_a]), jnp.stack([far_a, own_a]))
    a_p1, a_m1 = fetch(pa, dz=1), fetch(pa, dz=-1)
    y_b = jnp.stack(y_b)
    x_b = fetch(y_b, dx=1)
    from_chip = swap_tensor(gradient_later, 2)
    core_partial = swap_tensor(partial, 1)
    split = split_columns(from_core, place(1), row_count, split)

    a_p1, a_m1, x_b, core_partial, pa, y_b, *split = together(
        a_p1, a_m1, x_b, core_partial, pa, y_b, *split
    )
    a_p2, a_m2 = fetch(a_p1, dz=1), fetch(a_m1, dz=-1)
    c1 = jnp.stack([a_m1, pa, a_p1])
    f1_p, f1_m = fetch(c1, dy=1), fetch(c1, dy=-1)
    bq = jnp.broadcast_to(
        jnp.where(xl == 0, jnp.stack([own_b, far_b]), jnp.stack([far_b, own_b]))[:, None],
        (NX, NY, shard_rows, b_width),
    )
    for i, offset in enumerate((1, 3, 2)):
        for j, chunk in ((0, y_b[i]), (1, x_b[i])):
            at = (xl ^ j, (y + offset) % NY, jnp.int32(0), jnp.int32(0))
            bq = lax.dynamic_update_slice(bq, chunk[None, None], at)
    bq = bq.reshape(NX * NY * shard_rows, b_width)
    chip_sum = partial + core_partial
    a_p2, a_m2, bq = together(a_p2, a_m2, bq)
    b_p1, b_m1 = fetch(bq, dz=1), fetch(bq, dz=-1)

    a_p2, a_m2, f1_p, f1_m, b_p1, b_m1, from_chip, chip_sum = together(
        a_p2, a_m2, f1_p, f1_m, b_p1, b_m1, from_chip, chip_sum
    )
    a_p3, a_m3 = fetch(a_p2, dz=1), fetch(a_m2, dz=-1)
    c2 = jnp.stack([a_m2, a_p2])
    r3_p = fetch(flat([f1_p[:, 0], c2]), dy=1)
    r3_m = fetch(flat([f1_m[:, 1], c2]), dy=-1)
    from_both = swap_tensor(from_chip, 1)
    split = split_columns(from_chip, place(2), row_count, split)
    s1 = put(put(start_buffer(c1), f1_p, y + 1), f1_m, y + 3)
    a_p3, a_m3, b_p1, b_m1, from_both, chip_sum = together(
        a_p3, a_m3, b_p1, b_m1, from_both, chip_sum
    )
    b_p2, b_m2 = fetch(b_p1, dz=1), fetch(b_m1, dz=-1)
    chip_sum_far = swap_tensor(chip_sum, 2)
    split = split_columns(from_both, place(3), row_count, split)

    a_p3, a_m3, r3_p, r3_m, b_p2, b_m2, chip_sum_far, s1, *split = together(
        a_p3, a_m3, r3_p, r3_m, b_p2, b_m2, chip_sum_far, s1, *split
    )
    f1_o0, f2_p = unflat(r3_p, 3, 2)
    f1_o1, f2_m = unflat(r3_m, 3, 2)
    a_4 = fetch(a_p3, dz=1)
    c3 = jnp.stack([a_m3, a_p3])
    r4_p = fetch(flat([f2_p[:, 0], c3]), dy=1)
    r4_m = fetch(flat([f2_m[:, 1], c3]), dy=-1)
    b_p3, b_m3 = fetch(b_p2, dz=1), fetch(b_m2, dz=-1)
    gradients, by_z = split
    s1 = put_half(put_half(s1, f1_o0, y + 2, 0), f1_o1, y + 2, 1)
    s2 = put(put(start_buffer(c2), f2_p, y + 1), f2_m, y + 3)

    position = jnp.arange(row_count, dtype=jnp.int32)
    active_rows = position < tenant_group_counts[0]
    slot_lookup = jnp.arange(adapter_down_factors.shape[1], dtype=jnp.int32) // ADAPTER_RANK
    select_rows = (
        active_rows[:, None] & (slot_lookup[None, :] == (tenant_index % TEN_DEV)[:, None])
    ).astype(jnp.float32)
    adapter_input = ((chip_sum + chip_sum_far) * select_rows).astype(jnp.bfloat16)
    (adapter_input,) = together(adapter_input)
    adapter_backward = (contract(gradients, adapter_up_factors, 1, 1) * select_rows).astype(
        jnp.bfloat16
    )
    down_factor_gradient = ADAPTER_SCALE * contract(head_outputs, adapter_backward, 0, 0)
    up_factor_gradient = ADAPTER_SCALE * contract(adapter_input, gradients, 0, 0)

    b_total = product(
        ADAPTER_SCALE * contract(adapter_backward, adapter_down_factors[a_width:], 1, 1),
        [(by_z[0], bq), (by_z[1], b_p1), (by_z[7], b_m1), (by_z[2], b_p2), (by_z[6], b_m2)],
    )

    a_4, r4_p, r4_m, b_p3, b_m3, s1, s2, b_total, up_factor_gradient = together(
        a_4, r4_p, r4_m, b_p3, b_m3, s1, s2, b_total, up_factor_gradient
    )
    f2_o0, f3_p = unflat(r4_p, 2, 2)
    f2_o1, f3_m = unflat(r4_m, 2, 2)
    a_4 = a_4[None]
    r5_p = fetch(flat([f3_p[:, 0], a_4]), dy=1)
    r5_m = fetch(flat([f3_m[:, 1], a_4]), dy=-1)
    f4_o = fetch(a_4, dy=2)
    cut = bq.shape[0] // 2 // 16 * 16
    b_4a, b_4b = fetch(b_p3[:cut], dz=1), fetch(b_m3[cut:], dz=-1)

    b_total = product(b_total, [(by_z[3], b_p3), (by_z[5], b_m3)])
    a_total = product(
        ADAPTER_SCALE * contract(adapter_backward, adapter_down_factors[:a_width], 1, 1),
        [(by_z[7], s1[0]), (by_z[0], s1[1]), (by_z[1], s1[2])],
    )
    s2 = put_half(put_half(s2, f2_o0, y + 2, 0), f2_o1, y + 2, 1)
    s3 = put(put(start_buffer(c3), f3_p, y + 1), f3_m, y + 3)
    a_total = product(a_total, [(by_z[6], s2[0]), (by_z[2], s2[1])])

    r5_p, r5_m, f4_o, b_4a, b_4b, s3, a_total, b_total = together(
        r5_p, r5_m, f4_o, b_4a, b_4b, s3, a_total, b_total
    )
    f3_o0, f4_p = unflat(r5_p, 2, 1)
    f3_o1, f4_m = unflat(r5_m, 2, 1)
    s3 = put_half(put_half(s3, f3_o0, y + 2, 0), f3_o1, y + 2, 1)
    s4 = put(put(put(start_buffer(a_4), f4_p, y + 1), f4_m, y + 3), f4_o, y + 2)
    a_total = product(a_total, [(by_z[5], s3[0]), (by_z[3], s3[1]), (by_z[4], s4[0])])
    b_total = product(b_total, [(by_z[4], jnp.concatenate([b_4a, b_4b], 0))])
    head_feature_gradient = jnp.where(
        active_rows[:, None], jnp.concatenate([a_total, b_total], 1), 0.0
    ).astype(jnp.bfloat16)
    return (head_feature_gradient, down_factor_gradient, up_factor_gradient)


def solution(mesh):
    in_specs = (
        P("dp", "tensor"),
        P(("dp", "tensor"), None),
        P("dp", "tensor"),
        P("tensor", "dp"),
        P("dp", None),
        P("dp"),
        P("dp"),
    )
    out_specs = (P("dp", "tensor"), P("tensor", "dp"), P("dp", None))
    return jax.shard_map(body, mesh=mesh, in_specs=in_specs, out_specs=out_specs, check_vma=False)
```

```python
import jax
import jax.numpy as jnp
from jax import lax
from jax.experimental import pallas as pl
from jax.experimental.pallas import tpu as pltpu
from jax.sharding import PartitionSpec as P

ADAPTER_RANK = 16
TEN_DEV = 8
ADAPTER_SCALE = 2.0
NZ, NX, NY = 8, 2, 4


def contract(left, right, left_dim, right_dim):
    return lax.dot_general(
        left, right, (((left_dim,), (right_dim,)), ((), ())), preferred_element_type=jnp.float32
    )


def fetch(x, dz=0, dx=0, dy=0):
    pairs = []
    for z in range(NZ):
        for a in range(NX):
            for y in range(NY):
                source = (((z + dz) % NZ) * NX + (a + dx) % NX) * NY + (y + dy) % NY
                pairs.append((source, (z * NX + a) * NY + y))
    return lax.ppermute(x, "dp", pairs)


def swap_tensor(x, mask):
    return lax.ppermute(x, "tensor", [(t, t ^ mask) for t in range(4)])


def together(*values):
    return lax.optimization_barrier(values)


def split_kernel(start_ref, g_ref, out_ref):
    width = out_ref.shape[2]
    for block in range(NZ):
        slot = lax.rem(block - start_ref[0] + NZ, NZ)
        out_ref[slot] = g_ref[:, block * width : (block + 1) * width]


def split_columns(gradients, start):
    rows, depth = gradients.shape
    step = rows // 4
    width = depth // NZ
    return pl.pallas_call(
        split_kernel,
        grid_spec=pltpu.PrefetchScalarGridSpec(
            num_scalar_prefetch=1,
            grid=(4,),
            in_specs=[pl.BlockSpec((step, depth), lambda i, s: (i, 0))],
            out_specs=pl.BlockSpec((NZ, step, width), lambda i, s: (0, i, 0)),
        ),
        out_shape=jax.ShapeDtypeStruct((NZ, rows, width), gradients.dtype),
        compiler_params=pltpu.CompilerParams(vmem_limit_bytes=32 * 1024 * 1024),
    )(start, gradients)


def put(buffer, chunk, index):
    axis = buffer.ndim - 3
    return lax.dynamic_update_slice_in_dim(buffer, jnp.expand_dims(chunk, axis), index % NY, axis)


def in_y_order(chunks, y):
    own = chunks[0]
    buffer = jnp.broadcast_to(
        jnp.expand_dims(own, own.ndim - 2), own.shape[:-2] + (NY,) + own.shape[-2:]
    )
    for offset, chunk in chunks.items():
        if offset:
            buffer = put(buffer, chunk, y + offset)
    return buffer


def body(
    head_outputs,
    output_gradient,
    frozen_weight,
    adapter_down_factors,
    adapter_up_factors,
    tenant_index,
    tenant_group_counts,
):
    row_count = head_outputs.shape[0]
    shard_rows, feature_width = frozen_weight.shape
    a_width = feature_width * 5 // 8
    group = lax.axis_index("dp").astype(jnp.int32)
    z, xl, y = group // (NX * NY), (group // NY) % NX, group % NY

    other = fetch(frozen_weight, dx=1)
    gradients = lax.all_gather(output_gradient, "tensor", axis=0, tiled=True)
    partial = jnp.dot(head_outputs, adapter_down_factors, preferred_element_type=jnp.float32)
    core_partial = swap_tensor(partial, 1)

    def pair(columns):
        mine, far = frozen_weight[:, columns], other[:, columns]
        return jnp.where(xl == 0, jnp.stack([mine, far]), jnp.stack([far, mine]))

    pair_a, pair_b = pair(slice(0, a_width)), pair(slice(a_width, None))

    a_p1, a_m1 = fetch(pair_a, dz=1), fetch(pair_a, dz=-1)
    b_p, b_m, b_o = fetch(pair_b, dy=1), fetch(pair_b, dy=-1), fetch(pair_b, dy=2)

    a_p1, a_m1 = together(a_p1, a_m1)
    a_p2, a_m2 = fetch(a_p1, dz=1), fetch(a_m1, dz=-1)
    b_p, b_m, b_o, pair_b, a_p1, a_m1 = together(b_p, b_m, b_o, pair_b, a_p1, a_m1)
    b_own = in_y_order({0: pair_b, 1: b_p, 3: b_m, 2: b_o}, y)
    b_own = b_own.reshape(NX * NY * shard_rows, -1)
    b_p1, b_m1 = fetch(b_own, dz=1), fetch(b_own, dz=-1)

    a_p2, a_m2, b_own = together(a_p2, a_m2, b_own)
    a_p3, a_m3 = fetch(a_p2, dz=1), fetch(a_m2, dz=-1)
    first = jnp.stack([a_m1, pair_a, a_p1, a_p2])
    f_p, f_m = fetch(first, dy=1), fetch(first, dy=-1)
    partial, core_partial, first = together(partial, core_partial, first)
    chip_sum = partial + core_partial
    far_sum = swap_tensor(chip_sum, 2)

    a_p3, a_m3 = together(a_p3, a_m3)
    a_o = fetch(a_p3, dz=1)

    a_o, b_p1, b_m1 = together(a_o, b_p1, b_m1)
    b_p2, b_m2 = fetch(b_p1, dz=1), fetch(b_m1, dz=-1)
    second = jnp.stack([a_p3, a_o, a_m3, a_m2])

    f_p, f_m, second = together(f_p, f_m, second)
    f_o = fetch(f_m, dy=-1)
    s_p, s_m = fetch(second, dy=1), fetch(second, dy=-1)

    b_p2, b_m2, f_p, f_m = together(b_p2, b_m2, f_p, f_m)
    b_p3, b_m3 = fetch(b_p2, dz=1), fetch(b_m2, dz=-1)

    f_o, s_p, s_m, b_p2, gradients = together(f_o, s_p, s_m, b_p2, gradients)
    s_o = fetch(s_p, dy=1)
    by_z = split_columns(gradients, ((z + NZ - 1) % NZ).reshape(1))

    b_p3, b_m3, s_p, f_o, by_z = together(b_p3, b_m3, s_p, f_o, by_z)
    cut = b_own.shape[0] // 3 // 16 * 16
    b_o4 = [fetch(b_p3[:cut], dz=1), fetch(b_m3[cut:], dz=-1)]

    position = jnp.arange(row_count, dtype=jnp.int32)
    active_rows = position < tenant_group_counts[0]
    slot_lookup = jnp.arange(adapter_down_factors.shape[1], dtype=jnp.int32) // ADAPTER_RANK
    select_rows = (
        active_rows[:, None] & (slot_lookup[None, :] == (tenant_index % TEN_DEV)[:, None])
    ).astype(jnp.float32)
    adapter_input = ((chip_sum + far_sum) * select_rows).astype(jnp.bfloat16)
    (adapter_input,) = together(adapter_input)
    adapter_backward = (contract(gradients, adapter_up_factors, 1, 1) * select_rows).astype(
        jnp.bfloat16
    )
    down_factor_gradient = ADAPTER_SCALE * contract(head_outputs, adapter_backward, 0, 0)
    up_factor_gradient = ADAPTER_SCALE * contract(adapter_input, gradients, 0, 0)

    def product(total, terms):
        for slot, chunk in terms:
            total = total + contract(by_z[slot], chunk.reshape(by_z.shape[2], -1), 1, 0)
        return total

    first_all = in_y_order({0: first, 1: f_p, 3: f_m, 2: f_o}, y)
    second_all = in_y_order({0: second, 1: s_p, 3: s_m}, y)
    a_total = product(
        ADAPTER_SCALE * contract(adapter_backward, adapter_down_factors[:a_width], 1, 1),
        [(i, first_all[i]) for i in range(4)],
    )
    b_total = product(
        ADAPTER_SCALE * contract(adapter_backward, adapter_down_factors[a_width:], 1, 1),
        [(1, b_own), (0, b_m1), (2, b_p1), (7, b_m2), (3, b_p2), (6, b_m3), (4, b_p3)],
    )
    (
        s_o, b_p4, b_m4, second_all, a_total, b_total, down_factor_gradient, up_factor_gradient
    ) = together(
        s_o, *b_o4, second_all, a_total, b_total, down_factor_gradient, up_factor_gradient
    )
    second_all = put(second_all, s_o, y + 2)
    b_total = product(b_total, [(5, jnp.concatenate([b_p4, b_m4], 0))])
    a_total = product(a_total, [(4 + i, second_all[i]) for i in range(4)])
    head_feature_gradient = jnp.where(
        active_rows[:, None], jnp.concatenate([a_total, b_total], 1), 0.0
    ).astype(jnp.bfloat16)
    return (head_feature_gradient, down_factor_gradient, up_factor_gradient)


def solution(mesh):
    in_specs = (
        P("dp", "tensor"),
        P(("dp", "tensor"), None),
        P("dp", "tensor"),
        P("tensor", "dp"),
        P("dp", None),
        P("dp"),
        P("dp"),
    )
    out_specs = (P("dp", "tensor"), P("tensor", "dp"), P("dp", None))
    return jax.shard_map(body, mesh=mesh, in_specs=in_specs, out_specs=out_specs, check_vma=False)
```

```python
import jax
import jax.numpy as jnp
from jax import lax
from jax.experimental import pallas as pl
from jax.experimental.pallas import tpu as pltpu
from jax.sharding import PartitionSpec as P

ADAPTER_RANK = 16
TEN_DEV = 8
ADAPTER_SCALE = 2.0
NZ, NX, NY = 8, 2, 4


def contract(left, right, left_dim, right_dim):
    return lax.dot_general(
        left, right, (((left_dim,), (right_dim,)), ((), ())), preferred_element_type=jnp.float32
    )


def fetch(x, dz=0, dx=0, dy=0):
    pairs = []
    for z in range(NZ):
        for a in range(NX):
            for y in range(NY):
                source = (((z + dz) % NZ) * NX + (a + dx) % NX) * NY + (y + dy) % NY
                pairs.append((source, (z * NX + a) * NY + y))
    return lax.ppermute(x, "dp", pairs)


def swap_tensor(x, mask):
    return lax.ppermute(x, "tensor", [(t, t ^ mask) for t in range(4)])


def together(*values):
    return lax.optimization_barrier(values)


def split_kernel(start_ref, g_ref, z_ref, x_ref):
    width = z_ref.shape[2]
    half = width // NX
    for block in range(NZ):
        slot = lax.rem(block - start_ref[0] + NZ, NZ)
        z_ref[slot] = g_ref[:, block * width : (block + 1) * width]
        for x in range(NX):
            to, at = (x * NZ + block) * half, (block * NX + x) * half
            x_ref[:, to : to + half] = g_ref[:, at : at + half]


def split_columns(gradients, start):
    rows, depth = gradients.shape
    step = rows // 4
    width = depth // NZ
    return pl.pallas_call(
        split_kernel,
        grid_spec=pltpu.PrefetchScalarGridSpec(
            num_scalar_prefetch=1,
            grid=(4,),
            in_specs=[pl.BlockSpec((step, depth), lambda i, s: (i, 0))],
            out_specs=[
                pl.BlockSpec((NZ, step, width), lambda i, s: (0, i, 0)),
                pl.BlockSpec((step, depth), lambda i, s: (i, 0)),
            ],
        ),
        out_shape=[
            jax.ShapeDtypeStruct((NZ, rows, width), gradients.dtype),
            jax.ShapeDtypeStruct((rows, depth), gradients.dtype),
        ],
        compiler_params=pltpu.CompilerParams(vmem_limit_bytes=32 * 1024 * 1024),
    )(start, gradients)


def put(buffer, chunk, index):
    axis = buffer.ndim - 3
    return lax.dynamic_update_slice_in_dim(buffer, jnp.expand_dims(chunk, axis), index % NY, axis)


def in_y_order(chunks, y):
    own = chunks[0]
    buffer = jnp.broadcast_to(
        jnp.expand_dims(own, own.ndim - 2), own.shape[:-2] + (NY,) + own.shape[-2:]
    )
    for offset, chunk in chunks.items():
        if offset:
            buffer = put(buffer, chunk, y + offset)
    return buffer


def body(
    head_outputs,
    output_gradient,
    frozen_weight,
    adapter_down_factors,
    adapter_up_factors,
    tenant_index,
    tenant_group_counts,
):
    row_count = head_outputs.shape[0]
    part_rows, depth = output_gradient.shape
    shard_rows, feature_width = frozen_weight.shape
    a_width = feature_width * 3 // 4
    group = lax.axis_index("dp").astype(jnp.int32)
    z, xl, y = group // (NX * NY), (group // NY) % NX, group % NY
    tensor = lax.axis_index("tensor").astype(jnp.int32)

    other = fetch(frozen_weight, dx=1)
    from_core = swap_tensor(output_gradient, 1)
    partial = jnp.dot(head_outputs, adapter_down_factors, preferred_element_type=jnp.float32)
    core_partial = swap_tensor(partial, 1)

    def pair(columns):
        mine, far = frozen_weight[:, columns], other[:, columns]
        return jnp.where(xl == 0, jnp.stack([mine, far]), jnp.stack([far, mine]))

    pair_a, pair_b = together(pair(slice(0, a_width)), pair(slice(a_width, None)))
    rings = [
        [((k * NX + x) * NY) + j for k in range(NZ) for j in range(NY)] for x in range(NX)
    ]
    a_all = lax.all_gather(pair_a, "dp", axis=1, tiled=True, axis_index_groups=rings)
    a_all = a_all.reshape(depth, a_width)

    b_p, b_m, b_o = fetch(pair_b, dy=1), fetch(pair_b, dy=-1), fetch(pair_b, dy=2)
    gradient_later, pair_b = together(output_gradient, pair_b)
    from_chip = swap_tensor(gradient_later, 2)
    b_own = in_y_order({0: pair_b, 1: b_p, 3: b_m, 2: b_o}, y)
    b_own = b_own.reshape(NX * NY * shard_rows, -1)
    b_p1, b_m1 = fetch(b_own, dz=1), fetch(b_own, dz=-1)

    partial, core_partial, b_own = together(partial, core_partial, b_own)
    chip_sum = partial + core_partial
    far_sum = swap_tensor(chip_sum, 2)

    b_p1, b_m1, far_sum = together(b_p1, b_m1, far_sum)
    b_p2, b_m2 = fetch(b_p1, dz=1), fetch(b_m1, dz=-1)
    from_chip, b_p1, b_m1 = together(from_chip, b_p1, b_m1)
    from_both = swap_tensor(from_chip, 1)

    b_p2, b_m2, from_both = together(b_p2, b_m2, from_both)
    b_p3, b_m3 = fetch(b_p2, dz=1), fetch(b_m2, dz=-1)

    b_p3, b_m3 = together(b_p3, b_m3)
    cut = b_own.shape[0] // 2 // 16 * 16
    b_p4, b_m4 = fetch(b_p3[:cut], dz=1), fetch(b_m3[cut:], dz=-1)

    gradients = jnp.zeros((row_count, depth), output_gradient.dtype)
    for block, mask in ((output_gradient, 0), (from_core, 1), (from_chip, 2), (from_both, 3)):
        gradients = lax.dynamic_update_slice_in_dim(
            gradients, block, (tensor ^ mask) * part_rows, 0
        )
    by_z, by_x = split_columns(gradients, z.reshape(1))

    position = jnp.arange(row_count, dtype=jnp.int32)
    active_rows = position < tenant_group_counts[0]
    slot_lookup = jnp.arange(adapter_down_factors.shape[1], dtype=jnp.int32) // ADAPTER_RANK
    select_rows = (
        active_rows[:, None] & (slot_lookup[None, :] == (tenant_index % TEN_DEV)[:, None])
    ).astype(jnp.float32)
    adapter_input = ((chip_sum + far_sum) * select_rows).astype(jnp.bfloat16)
    (adapter_input,) = together(adapter_input)
    adapter_backward = (contract(gradients, adapter_up_factors, 1, 1) * select_rows).astype(
        jnp.bfloat16
    )
    down_factor_gradient = ADAPTER_SCALE * contract(head_outputs, adapter_backward, 0, 0)
    up_factor_gradient = ADAPTER_SCALE * contract(adapter_input, gradients, 0, 0)

    a_total = ADAPTER_SCALE * contract(adapter_backward, adapter_down_factors[:a_width], 1, 1)
    b_total = ADAPTER_SCALE * contract(adapter_backward, adapter_down_factors[a_width:], 1, 1)
    chunks = (b_own, b_p1, b_p2, b_p3, jnp.concatenate([b_p4, b_m4], 0), b_m3, b_m2, b_m1)
    for slot in (0, 1, 7, 2, 6, 3, 5, 4):
        b_total = b_total + contract(by_z[slot], chunks[slot], 1, 0)
    live = active_rows[:, None]
    b_out = jnp.where(live, b_total, 0.0).astype(jnp.bfloat16)

    a_all, a_total, b_out, by_x, down_factor_gradient, up_factor_gradient = together(
        a_all, a_total, b_out, by_x, down_factor_gradient, up_factor_gradient
    )
    a_total = a_total + contract(by_x, a_all, 1, 0)
    a_out = jnp.where(live, a_total, 0.0).astype(jnp.bfloat16)
    return (jnp.concatenate([a_out, b_out], 1), down_factor_gradient, up_factor_gradient)


def solution(mesh):
    in_specs = (
        P("dp", "tensor"),
        P(("dp", "tensor"), None),
        P("dp", "tensor"),
        P("tensor", "dp"),
        P("dp", None),
        P("dp"),
        P("dp"),
    )
    out_specs = (P("dp", "tensor"), P("tensor", "dp"), P("dp", None))
    return jax.shard_map(body, mesh=mesh, in_specs=in_specs, out_specs=out_specs, check_vma=False)
```

```python
import jax
import jax.numpy as jnp
from jax import lax
from jax.experimental import pallas as pl
from jax.experimental.pallas import tpu as pltpu
from jax.sharding import PartitionSpec as P

ADAPTER_RANK = 16
TEN_DEV = 8
ADAPTER_SCALE = 2.0
NZ, NX, NY = 8, 2, 4


def contract(left, right, left_dim, right_dim):
    return lax.dot_general(
        left, right, (((left_dim,), (right_dim,)), ((), ())), preferred_element_type=jnp.float32
    )


def fetch(x, dz=0, dx=0, dy=0):
    pairs = []
    for z in range(NZ):
        for a in range(NX):
            for y in range(NY):
                source = (((z + dz) % NZ) * NX + (a + dx) % NX) * NY + (y + dy) % NY
                pairs.append((source, (z * NX + a) * NY + y))
    return lax.ppermute(x, "dp", pairs)


def swap_tensor(x, mask):
    return lax.ppermute(x, "tensor", [(t, t ^ mask) for t in range(4)])


def together(*values):
    return lax.optimization_barrier(values)


def split_kernel(start_ref, g_ref, z_ref):
    width = z_ref.shape[2]
    for block in range(NZ):
        slot = lax.rem(block - start_ref[0] + NZ, NZ)
        z_ref[slot] = g_ref[:, block * width : (block + 1) * width]


def split_columns(gradients, start):
    rows, depth = gradients.shape
    step = rows // 4
    width = depth // NZ
    return pl.pallas_call(
        split_kernel,
        grid_spec=pltpu.PrefetchScalarGridSpec(
            num_scalar_prefetch=1,
            grid=(4,),
            in_specs=[pl.BlockSpec((step, depth), lambda i, s: (i, 0))],
            out_specs=pl.BlockSpec((NZ, step, width), lambda i, s: (0, i, 0)),
        ),
        out_shape=jax.ShapeDtypeStruct((NZ, rows, width), gradients.dtype),
        compiler_params=pltpu.CompilerParams(vmem_limit_bytes=32 * 1024 * 1024),
    )(start, gradients)


def last_kernel(g_ref, w_ref, back_ref, down_ref, live_ref, b_ref, out_ref, total_ref):
    step = pl.program_id(0)
    width = w_ref.shape[1]

    @pl.when(step == 0)
    def _():
        total_ref[...] = ADAPTER_SCALE * contract(back_ref[...], down_ref[...], 1, 1)

    total_ref[...] += contract(g_ref[...], w_ref[...], 1, 0)

    @pl.when(step == pl.num_programs(0) - 1)
    def _():
        out_ref[:, :width] = jnp.where(live_ref[...] > 0, total_ref[...], 0.0).astype(
            out_ref.dtype
        )
        out_ref[:, width:] = b_ref[...]


def last_product(gradients, weight, back, down, live, b_out, steps=6):
    rows, depth = gradients.shape
    width = weight.shape[1]
    total = width + b_out.shape[1]
    block = depth // steps

    def whole(array):
        return pl.BlockSpec(array.shape, lambda i: (0, 0))

    return pl.pallas_call(
        last_kernel,
        grid=(steps,),
        in_specs=[
            pl.BlockSpec((rows, block), lambda i: (0, i)),
            pl.BlockSpec((block, width), lambda i: (i, 0)),
            whole(back),
            whole(down),
            whole(live),
            whole(b_out),
        ],
        out_specs=pl.BlockSpec((rows, total), lambda i: (0, 0)),
        out_shape=jax.ShapeDtypeStruct((rows, total), b_out.dtype),
        scratch_shapes=[pltpu.VMEM((rows, width), jnp.float32)],
        compiler_params=pltpu.CompilerParams(vmem_limit_bytes=32 * 1024 * 1024),
    )(gradients, weight, back, down, live, b_out)


def put(buffer, chunk, index):
    axis = buffer.ndim - 3
    return lax.dynamic_update_slice_in_dim(buffer, jnp.expand_dims(chunk, axis), index % NY, axis)


def in_y_order(chunks, y):
    own = chunks[0]
    buffer = jnp.broadcast_to(
        jnp.expand_dims(own, own.ndim - 2), own.shape[:-2] + (NY,) + own.shape[-2:]
    )
    for offset, chunk in chunks.items():
        if offset:
            buffer = put(buffer, chunk, y + offset)
    return buffer


def body(
    head_outputs,
    output_gradient,
    frozen_weight,
    adapter_down_factors,
    adapter_up_factors,
    tenant_index,
    tenant_group_counts,
):
    row_count = head_outputs.shape[0]
    part_rows, depth = output_gradient.shape
    shard_rows, feature_width = frozen_weight.shape
    a_width = feature_width // 2
    group = lax.axis_index("dp").astype(jnp.int32)
    z, xl, y = group // (NX * NY), (group // NY) % NX, group % NY
    tensor = lax.axis_index("tensor").astype(jnp.int32)

    other = fetch(frozen_weight, dx=1)

    def pair(columns):
        mine, far = frozen_weight[:, columns], other[:, columns]
        return jnp.where(xl == 0, jnp.stack([mine, far]), jnp.stack([far, mine]))

    pair_a, pair_b = pair(slice(0, a_width)), pair(slice(a_width, None))

    a_p1, a_m1 = fetch(pair_a, dz=1), fetch(pair_a, dz=-1)
    gradient_later, pair_a = together(output_gradient, pair_a)
    from_chip = swap_tensor(gradient_later, 2)
    a_p1, a_m1 = together(a_p1, a_m1)
    a_p2, a_m2 = fetch(a_p1, dz=1), fetch(a_m1, dz=-1)
    a_p2, a_m2, pair_b = together(a_p2, a_m2, pair_b)
    a_p3, a_m3 = fetch(a_p2, dz=1), fetch(a_m2, dz=-1)
    b_p, b_m, b_o = fetch(pair_b, dy=1), fetch(pair_b, dy=-1), fetch(pair_b, dy=2)
    b_p, b_m, b_o, a_p2 = together(b_p, b_m, b_o, a_p2)
    b_own = in_y_order({0: pair_b, 1: b_p, 3: b_m, 2: b_o}, y)
    b_own = b_own.reshape(NX * NY * shard_rows, -1)
    a_p3, a_m3, b_own = together(a_p3, a_m3, b_own)
    a_p4 = fetch(a_p3, dz=1)
    b_p1, b_m1 = fetch(b_own, dz=1), fetch(b_own, dz=-1)

    a_own = jnp.broadcast_to(pair_a[None], (NZ,) + pair_a.shape)
    for dz, chunk in ((1, a_p1), (7, a_m1), (2, a_p2), (6, a_m2), (3, a_p3), (5, a_m3), (4, a_p4)):
        a_own = lax.dynamic_update_slice_in_dim(a_own, chunk[None], (z + dz) % NZ, 0)
    rings = [[first + j for j in range(NY)] for first in range(0, NZ * NX * NY, NY)]
    a_all = lax.all_gather(
        a_own[:, :, None], "dp", axis=2, tiled=True, axis_index_groups=rings
    ).reshape(depth, a_width)

    b_p1, b_m1, from_chip, head_later, own_rows = together(
        b_p1, b_m1, from_chip, head_outputs, output_gradient
    )
    b_p2, b_m2 = fetch(b_p1, dz=1), fetch(b_m1, dz=-1)
    from_core = swap_tensor(own_rows, 1)
    from_both = swap_tensor(from_chip, 1)
    partial = jnp.dot(head_later, adapter_down_factors, preferred_element_type=jnp.float32)
    core_partial = swap_tensor(partial, 1)

    b_p2, b_m2, from_both, from_core, partial, core_partial = together(
        b_p2, b_m2, from_both, from_core, partial, core_partial
    )
    b_p3, b_m3 = fetch(b_p2, dz=1), fetch(b_m2, dz=-1)
    chip_sum = partial + core_partial
    far_sum = swap_tensor(chip_sum, 2)

    b_p3, b_m3, far_sum = together(b_p3, b_m3, far_sum)
    cut = b_own.shape[0] // 2 // 16 * 16
    b_p4, b_m4 = fetch(b_p3[:cut], dz=1), fetch(b_m3[cut:], dz=-1)

    gradients = jnp.zeros((row_count, depth), output_gradient.dtype)
    for block, mask in ((own_rows, 0), (from_core, 1), (from_chip, 2), (from_both, 3)):
        gradients = lax.dynamic_update_slice_in_dim(
            gradients, block, (tensor ^ mask) * part_rows, 0
        )
    by_z = split_columns(gradients, z.reshape(1))

    position = jnp.arange(row_count, dtype=jnp.int32)
    active_rows = position < tenant_group_counts[0]
    slot_lookup = jnp.arange(adapter_down_factors.shape[1], dtype=jnp.int32) // ADAPTER_RANK
    select_rows = (
        active_rows[:, None] & (slot_lookup[None, :] == (tenant_index % TEN_DEV)[:, None])
    ).astype(jnp.float32)
    adapter_input = ((chip_sum + far_sum) * select_rows).astype(jnp.bfloat16)
    (adapter_input,) = together(adapter_input)
    adapter_backward = (contract(gradients, adapter_up_factors, 1, 1) * select_rows).astype(
        jnp.bfloat16
    )
    down_factor_gradient = ADAPTER_SCALE * contract(head_outputs, adapter_backward, 0, 0)
    up_factor_gradient = ADAPTER_SCALE * contract(adapter_input, gradients, 0, 0)

    b_total = ADAPTER_SCALE * contract(adapter_backward, adapter_down_factors[a_width:], 1, 1)
    chunks = (b_own, b_p1, b_p2, b_p3, jnp.concatenate([b_p4, b_m4], 0), b_m3, b_m2, b_m1)
    for slot in (0, 1, 7, 2, 6, 3, 5, 4):
        b_total = b_total + contract(by_z[slot], chunks[slot], 1, 0)
    b_out = jnp.where(active_rows[:, None], b_total, 0.0).astype(jnp.bfloat16)
    live = active_rows.astype(jnp.float32)[:, None]

    a_all, b_out, live, adapter_backward, down_factor_gradient, up_factor_gradient = together(
        a_all, b_out, live, adapter_backward, down_factor_gradient, up_factor_gradient
    )
    head_feature_gradient = last_product(
        gradients, a_all, adapter_backward, adapter_down_factors[:a_width], live, b_out
    )
    return (head_feature_gradient, down_factor_gradient, up_factor_gradient)


def solution(mesh):
    in_specs = (
        P("dp", "tensor"),
        P(("dp", "tensor"), None),
        P("dp", "tensor"),
        P("tensor", "dp"),
        P("dp", None),
        P("dp"),
        P("dp"),
    )
    out_specs = (P("dp", "tensor"), P("tensor", "dp"), P("dp", None))
    return jax.shard_map(body, mesh=mesh, in_specs=in_specs, out_specs=out_specs, check_vma=False)
```

```python
import jax
import jax.numpy as jnp
from jax import lax
from jax.experimental import pallas as pl
from jax.experimental.pallas import tpu as pltpu
from jax.sharding import PartitionSpec as P

ADAPTER_RANK = 16
TEN_DEV = 8
ADAPTER_SCALE = 2.0
NZ, NX, NY = 8, 2, 4


def contract(left, right, left_dim, right_dim):
    return lax.dot_general(
        left, right, (((left_dim,), (right_dim,)), ((), ())), preferred_element_type=jnp.float32
    )


def fetch(x, dz=0, dx=0, dy=0):
    pairs = []
    for z in range(NZ):
        for a in range(NX):
            for y in range(NY):
                source = (((z + dz) % NZ) * NX + (a + dx) % NX) * NY + (y + dy) % NY
                pairs.append((source, (z * NX + a) * NY + y))
    return lax.ppermute(x, "dp", pairs)


def swap_tensor(x, mask):
    return lax.ppermute(x, "tensor", [(t, t ^ mask) for t in range(4)])


def together(*values):
    return lax.optimization_barrier(values)


def split_kernel(start_ref, g_ref, z_ref):
    width = z_ref.shape[2]
    for block in range(NZ):
        slot = lax.rem(block - start_ref[0] + NZ, NZ)
        z_ref[slot] = g_ref[:, block * width : (block + 1) * width]


def split_columns(gradients, start):
    rows, depth = gradients.shape
    step = rows // 4
    width = depth // NZ
    return pl.pallas_call(
        split_kernel,
        grid_spec=pltpu.PrefetchScalarGridSpec(
            num_scalar_prefetch=1,
            grid=(4,),
            in_specs=[pl.BlockSpec((step, depth), lambda i, s: (i, 0))],
            out_specs=pl.BlockSpec((NZ, step, width), lambda i, s: (0, i, 0)),
        ),
        out_shape=jax.ShapeDtypeStruct((NZ, rows, width), gradients.dtype),
        compiler_params=pltpu.CompilerParams(vmem_limit_bytes=32 * 1024 * 1024),
    )(start, gradients)


def last_kernel(g_ref, w_ref, back_ref, down_ref, live_ref, b_ref, out_ref):
    width = w_ref.shape[1]
    total = contract(g_ref[...], w_ref[...], 1, 0)
    total += ADAPTER_SCALE * contract(back_ref[...], down_ref[...], 1, 1)
    out_ref[:, :width] = jnp.where(live_ref[...] > 0, total, 0.0).astype(out_ref.dtype)
    out_ref[:, width:] = b_ref[...]


def down_kernel(head_ref, back_ref, out_ref):
    out_ref[...] = ADAPTER_SCALE * contract(head_ref[...], back_ref[...], 0, 0)


def in_vmem(kernel, shape, dtype, *arrays):
    return pl.pallas_call(
        kernel,
        in_specs=[pl.BlockSpec(memory_space=pltpu.VMEM)] * len(arrays),
        out_specs=pl.BlockSpec(memory_space=pltpu.VMEM),
        out_shape=jax.ShapeDtypeStruct(shape, dtype),
        compiler_params=pltpu.CompilerParams(vmem_limit_bytes=40 * 1024 * 1024),
    )(*arrays)


def body(
    head_outputs,
    output_gradient,
    frozen_weight,
    adapter_down_factors,
    adapter_up_factors,
    tenant_index,
    tenant_group_counts,
):
    row_count = head_outputs.shape[0]
    part_rows, depth = output_gradient.shape
    shard_rows, feature_width = frozen_weight.shape
    a_width = feature_width // 2
    group = lax.axis_index("dp").astype(jnp.int32)
    z, xl, y = group // (NX * NY), (group // NY) % NX, group % NY
    tensor = lax.axis_index("tensor").astype(jnp.int32)

    own_a, own_b = frozen_weight[:, :a_width], frozen_weight[:, a_width:]
    other = fetch(frozen_weight, dx=1)
    y_b = [fetch(own_b, dy=dy) for dy in (1, 2, 3)]
    from_core = swap_tensor(output_gradient, 1)
    other, from_core, *y_b = together(other, from_core, *y_b)

    far_a, far_b = other[:, :a_width], other[:, a_width:]
    pair_a = jnp.where(xl == 0, jnp.stack([own_a, far_a]), jnp.stack([far_a, own_a]))
    a_p1, a_m1 = fetch(pair_a, dz=1), fetch(pair_a, dz=-1)
    y_b = jnp.stack(y_b)
    x_b = fetch(y_b, dx=1)
    gradient_later, head_later, pair_a, y_b = together(
        output_gradient, head_outputs, pair_a, y_b
    )
    from_chip = swap_tensor(gradient_later, 2)
    partial = jnp.dot(head_later, adapter_down_factors, preferred_element_type=jnp.float32)
    core_partial = swap_tensor(partial, 1)
    a_p1, a_m1, x_b = together(a_p1, a_m1, x_b)
    a_p2, a_m2 = fetch(a_p1, dz=1), fetch(a_m1, dz=-1)
    b_own = jnp.broadcast_to(
        jnp.where(xl == 0, jnp.stack([own_b, far_b]), jnp.stack([far_b, own_b]))[:, None],
        (NX, NY, shard_rows, own_b.shape[1]),
    )
    zero = jnp.int32(0)
    for i, dy in enumerate((1, 2, 3)):
        for x, chunk in ((xl, y_b[i]), (1 - xl, x_b[i])):
            b_own = lax.dynamic_update_slice(
                b_own, chunk[None, None], (x, (y + dy) % NY, zero, zero)
            )
    b_own = b_own.reshape(NX * NY * shard_rows, -1)
    b_p1, b_m1 = fetch(b_own, dz=1), fetch(b_own, dz=-1)
    a_p2, a_m2, b_own = together(a_p2, a_m2, b_own)
    a_p3, a_m3 = fetch(a_p2, dz=1), fetch(a_m2, dz=-1)
    a_p3, a_m3 = together(a_p3, a_m3)
    a_p4 = fetch(a_p3, dz=1)

    b_p1, b_m1, a_p3, a_m3 = together(b_p1, b_m1, a_p3, a_m3)
    b_p2, b_m2 = fetch(b_p1, dz=1), fetch(b_m1, dz=-1)

    a_own = jnp.broadcast_to(pair_a[None], (NZ,) + pair_a.shape)
    for dz, chunk in ((1, a_p1), (7, a_m1), (2, a_p2), (6, a_m2), (3, a_p3), (5, a_m3), (4, a_p4)):
        a_own = lax.dynamic_update_slice_in_dim(a_own, chunk[None], (z + dz) % NZ, 0)
    half = NZ // 2
    a_low, a_high = together(a_own[:half], a_own[half:])
    low_p, low_m = fetch(a_low, dy=1), fetch(a_low, dy=-1)

    from_chip, a_low, a_high = together(from_chip, a_low, a_high)
    from_both = swap_tensor(from_chip, 1)

    b_p2, b_m2, low_p, low_m, from_both, partial, core_partial = together(
        b_p2, b_m2, low_p, low_m, from_both, partial, core_partial
    )
    b_p3, b_m3 = fetch(b_p2, dz=1), fetch(b_m2, dz=-1)
    high_p, high_m, low_o = fetch(a_high, dy=1), fetch(a_high, dy=-1), fetch(low_p, dy=1)

    gradients = jnp.zeros((row_count, depth), output_gradient.dtype)
    for block, mask in ((output_gradient, 0), (from_core, 1), (from_chip, 2), (from_both, 3)):
        gradients = lax.dynamic_update_slice_in_dim(
            gradients, block, (tensor ^ mask) * part_rows, 0
        )
    chip_sum = partial + core_partial
    far_sum = swap_tensor(chip_sum, 2)
    by_z = split_columns(gradients, z.reshape(1))

    b_p3, b_m3, high_p, high_m, low_o, by_z, far_sum = together(
        b_p3, b_m3, high_p, high_m, low_o, by_z, far_sum
    )
    cut = b_own.shape[0] // 2 // 16 * 16
    b_p4, b_m4 = fetch(b_p3[:cut], dz=1), fetch(b_m3[cut:], dz=-1)
    high_o = fetch(high_m, dy=-1)

    position = jnp.arange(row_count, dtype=jnp.int32)
    active_rows = position < tenant_group_counts[0]
    slot_lookup = jnp.arange(adapter_down_factors.shape[1], dtype=jnp.int32) // ADAPTER_RANK
    select_rows = (
        active_rows[:, None] & (slot_lookup[None, :] == (tenant_index % TEN_DEV)[:, None])
    ).astype(jnp.float32)
    adapter_input = ((chip_sum + far_sum) * select_rows).astype(jnp.bfloat16)
    adapter_backward = (contract(gradients, adapter_up_factors, 1, 1) * select_rows).astype(
        jnp.bfloat16
    )
    down_factor_gradient = in_vmem(
        down_kernel, adapter_down_factors.shape, jnp.float32, head_outputs, adapter_backward
    )

    b_total = ADAPTER_SCALE * contract(adapter_backward, adapter_down_factors[a_width:], 1, 1)
    chunks = (b_own, b_p1, b_p2, b_p3, None, b_m3, b_m2, b_m1)
    for slot in (0, 1, 7, 2, 6, 3, 5):
        b_total = b_total + contract(by_z[slot], chunks[slot], 1, 0)
    live = active_rows.astype(jnp.float32)[:, None]

    adapter_input, b_p4, b_m4, *arrived = together(
        adapter_input, b_p4, b_m4, a_low, low_p, low_m, low_o, a_high, high_p, high_m
    )
    up_factor_gradient = ADAPTER_SCALE * contract(adapter_input, gradients, 0, 0)
    b_total = b_total + contract(by_z[4], jnp.concatenate([b_p4, b_m4], 0), 1, 0)
    b_out = jnp.where(active_rows[:, None], b_total, 0.0).astype(jnp.bfloat16)
    a_all = jnp.zeros((NZ, NX, NY) + a_own.shape[2:], a_own.dtype)

    def placed(array, chunk, first, dy):
        at = (jnp.int32(first), zero, (y + dy) % NY, zero, zero)
        return lax.dynamic_update_slice(array, chunk[:, :, None], at)

    places = ((0, 0), (0, 1), (0, 3), (0, 2), (half, 0), (half, 1), (half, 3))
    for (first, dy), chunk in zip(places, arrived):
        a_all = placed(a_all, chunk, first, dy)

    high_o, a_all, b_out, down_factor_gradient, up_factor_gradient = together(
        high_o, a_all, b_out, down_factor_gradient, up_factor_gradient
    )
    a_all = placed(a_all, high_o, half, 2)
    head_feature_gradient = in_vmem(
        last_kernel,
        head_outputs.shape,
        jnp.bfloat16,
        gradients,
        a_all.reshape(depth, a_width),
        adapter_backward,
        adapter_down_factors[:a_width],
        live,
        b_out,
    )
    return (head_feature_gradient, down_factor_gradient, up_factor_gradient)


def solution(mesh):
    in_specs = (
        P("dp", "tensor"),
        P(("dp", "tensor"), None),
        P("dp", "tensor"),
        P("tensor", "dp"),
        P("dp", None),
        P("dp"),
        P("dp"),
    )
    out_specs = (P("dp", "tensor"), P("tensor", "dp"), P("dp", None))
    return jax.shard_map(body, mesh=mesh, in_specs=in_specs, out_specs=out_specs, check_vma=False)
```

```python
import jax
import jax.numpy as jnp
from jax import lax
from jax.experimental import pallas as pl
from jax.experimental.pallas import tpu as pltpu
from jax.sharding import PartitionSpec as P

ADAPTER_RANK = 16
TEN_DEV = 8
ADAPTER_SCALE = 2.0
NZ, NX, NY = 8, 2, 4


def contract(left, right, left_dim, right_dim):
    return lax.dot_general(
        left, right, (((left_dim,), (right_dim,)), ((), ())), preferred_element_type=jnp.float32
    )


def fetch(x, dz=0, dx=0, dy=0):
    pairs = []
    for z in range(NZ):
        for a in range(NX):
            for y in range(NY):
                source = (((z + dz) % NZ) * NX + (a + dx) % NX) * NY + (y + dy) % NY
                pairs.append((source, (z * NX + a) * NY + y))
    return lax.ppermute(x, "dp", pairs)


def swap_tensor(x, mask):
    return lax.ppermute(x, "tensor", [(t, t ^ mask) for t in range(4)])


def together(*values):
    return lax.optimization_barrier(values)


def split_kernel(start_ref, g_ref, z_ref):
    width = z_ref.shape[2]
    for block in range(NZ):
        slot = lax.rem(block - start_ref[0] + NZ, NZ)
        z_ref[slot] = g_ref[:, block * width : (block + 1) * width]


def split_columns(gradients, start):
    rows, depth = gradients.shape
    step = rows // 4
    width = depth // NZ
    return pl.pallas_call(
        split_kernel,
        grid_spec=pltpu.PrefetchScalarGridSpec(
            num_scalar_prefetch=1,
            grid=(4,),
            in_specs=[pl.BlockSpec((step, depth), lambda i, s: (i, 0))],
            out_specs=pl.BlockSpec((NZ, step, width), lambda i, s: (0, i, 0)),
        ),
        out_shape=jax.ShapeDtypeStruct((NZ, rows, width), gradients.dtype),
        compiler_params=pltpu.CompilerParams(vmem_limit_bytes=32 * 1024 * 1024),
    )(start, gradients)


def last_kernel(z_ref, w_ref, total_ref, live_ref, b_ref, out_ref):
    width = w_ref.shape[2]
    count = w_ref.shape[0]
    total = total_ref[...]
    for i in range(count):
        total += contract(z_ref[NZ - count + i], w_ref[i], 1, 0)
    out_ref[:, :width] = jnp.where(live_ref[...] > 0, total, 0.0).astype(out_ref.dtype)
    out_ref[:, width:] = b_ref[...]


def down_kernel(head_ref, back_ref, out_ref):
    out_ref[...] = ADAPTER_SCALE * contract(head_ref[...], back_ref[...], 0, 0)


def in_vmem(kernel, shape, dtype, *arrays):
    return pl.pallas_call(
        kernel,
        in_specs=[pl.BlockSpec(memory_space=pltpu.VMEM)] * len(arrays),
        out_specs=pl.BlockSpec(memory_space=pltpu.VMEM),
        out_shape=jax.ShapeDtypeStruct(shape, dtype),
        compiler_params=pltpu.CompilerParams(vmem_limit_bytes=40 * 1024 * 1024),
    )(*arrays)


def body(
    head_outputs,
    output_gradient,
    frozen_weight,
    adapter_down_factors,
    adapter_up_factors,
    tenant_index,
    tenant_group_counts,
):
    row_count = head_outputs.shape[0]
    part_rows, depth = output_gradient.shape
    shard_rows, feature_width = frozen_weight.shape
    a_width = feature_width * 5 // 8
    group = lax.axis_index("dp").astype(jnp.int32)
    z, xl, y = group // (NX * NY), (group // NY) % NX, group % NY
    tensor = lax.axis_index("tensor").astype(jnp.int32)
    zero = jnp.int32(0)

    own_a, own_b = frozen_weight[:, :a_width], frozen_weight[:, a_width:]
    other = fetch(frozen_weight, dx=1)
    y_b = [fetch(own_b, dy=dy) for dy in (1, 2, 3)]
    from_core = swap_tensor(output_gradient, 1)
    other, from_core, own_rows, head_later, index_later, *y_b = together(
        other, from_core, output_gradient, head_outputs, tenant_index, *y_b
    )

    far_a, far_b = other[:, :a_width], other[:, a_width:]
    pair_a = jnp.where(xl == 0, jnp.stack([own_a, far_a]), jnp.stack([far_a, own_a]))
    a_p1, a_m1 = fetch(pair_a, dz=1), fetch(pair_a, dz=-1)
    y_b = jnp.stack(y_b)
    x_b = fetch(y_b, dx=1)
    y_b, pair_a, gradient_later, head_later = together(y_b, pair_a, own_rows, head_later)
    from_chip = swap_tensor(gradient_later, 2)
    partial = jnp.dot(head_later, adapter_down_factors, preferred_element_type=jnp.float32)
    core_partial = swap_tensor(partial, 1)

    a_p1, a_m1, x_b, pair_a, partial, core_partial = together(
        a_p1, a_m1, x_b, pair_a, partial, core_partial
    )
    a_p2, a_m2 = fetch(a_p1, dz=1), fetch(a_m1, dz=-1)
    a_p4 = fetch(pair_a, dz=4)
    b_own = jnp.broadcast_to(
        jnp.where(xl == 0, jnp.stack([own_b, far_b]), jnp.stack([far_b, own_b]))[:, None],
        (NX, NY, shard_rows, own_b.shape[1]),
    )
    for i, dy in enumerate((1, 2, 3)):
        for x, chunk in ((xl, y_b[i]), (1 - xl, x_b[i])):
            b_own = lax.dynamic_update_slice(
                b_own, chunk[None, None], (x, (y + dy) % NY, zero, zero)
            )
    b_own = b_own.reshape(NX * NY * shard_rows, -1)

    a_p2, a_m2, b_own = together(a_p2, a_m2, b_own)
    a_p3, a_m3 = fetch(a_p2, dz=1), fetch(a_m2, dz=-1)
    low = jnp.stack([a_m1, pair_a, a_p1, a_p2])
    low_p, low_m = fetch(low, dy=1), fetch(low, dy=-1)

    a_p3, a_m3, a_p4, b_own = together(a_p3, a_m3, a_p4, b_own)
    high = jnp.stack([a_p3, a_p4, a_m3, a_m2])
    b_p1, b_m1 = fetch(b_own, dz=1), fetch(b_own, dz=-1)

    chip_sum = partial + core_partial
    far_sum = swap_tensor(chip_sum, 2)
    b_p1, b_m1, low_p, low_m, high, from_chip, own_rows, far_sum = together(
        b_p1, b_m1, low_p, low_m, high, from_chip, own_rows, far_sum
    )
    b_p2, b_m2 = fetch(b_p1, dz=1), fetch(b_m1, dz=-1)
    low_o, high_m = fetch(low_p, dy=1), fetch(high, dy=-1)

    from_both = swap_tensor(from_chip, 1)
    gradients = jnp.zeros((row_count, depth), output_gradient.dtype)
    for block, mask in ((own_rows, 0), (from_core, 1), (from_chip, 2), (from_both, 3)):
        gradients = lax.dynamic_update_slice_in_dim(
            gradients, block, (tensor ^ mask) * part_rows, 0
        )

    def placed(array, chunk, dy):
        return lax.dynamic_update_slice_in_dim(array, chunk[:, :, None], (y + dy) % NY, 2)

    def spread(chunk):
        return jnp.broadcast_to(chunk[:, :, None], (chunk.shape[0], NX, NY) + chunk.shape[2:])

    low_all = placed(placed(spread(low), low_p, 1), low_m, 3)

    b_p2, b_m2, gradients = together(b_p2, b_m2, gradients)
    b_p3, b_m3 = fetch(b_p2, dz=1), fetch(b_m2, dz=-1)
    low_o, high_m, high, low_all, b_p2 = together(low_o, high_m, high, low_all, b_p2)
    high_p, high_o = fetch(high, dy=1), fetch(high_m, dy=-1)
    by_z = split_columns(gradients, ((z + NZ - 1) % NZ).reshape(1))

    position = jnp.arange(row_count, dtype=jnp.int32)
    active_rows = position < tenant_group_counts[0]
    slot_lookup = jnp.arange(adapter_down_factors.shape[1], dtype=jnp.int32) // ADAPTER_RANK
    select_rows = (
        active_rows[:, None] & (slot_lookup[None, :] == (index_later % TEN_DEV)[:, None])
    ).astype(jnp.float32)
    adapter_backward = (contract(gradients, adapter_up_factors, 1, 1) * select_rows).astype(
        jnp.bfloat16
    )
    down_factor_gradient = in_vmem(
        down_kernel, adapter_down_factors.shape, jnp.float32, head_outputs, adapter_backward
    )
    live = active_rows.astype(jnp.float32)[:, None]

    b_p3, b_m3, by_z, adapter_backward, down_factor_gradient = together(
        b_p3, b_m3, by_z, adapter_backward, down_factor_gradient
    )
    cut = b_own.shape[0] // 2 // 16 * 16
    b_p4, b_m4 = fetch(b_p3[:cut], dz=1), fetch(b_m3[cut:], dz=-1)
    adapter_input = ((chip_sum + far_sum) * select_rows).astype(jnp.bfloat16)
    (adapter_input,) = together(adapter_input)
    up_factor_gradient = ADAPTER_SCALE * contract(adapter_input, gradients, 0, 0)

    def product(total, terms):
        for slot, chunk in terms:
            total = total + contract(by_z[slot], chunk.reshape(by_z.shape[2], -1), 1, 0)
        return total

    b_p4, b_m4, up_factor_gradient, low_all, high_m = together(
        b_p4, b_m4, up_factor_gradient, low_all, high_m
    )
    b_total = product(
        ADAPTER_SCALE * contract(adapter_backward, adapter_down_factors[a_width:], 1, 1),
        [(1, b_own), (0, b_m1), (2, b_p1), (7, b_m2), (3, b_p2), (6, b_m3), (4, b_p3)]
        + [(5, jnp.concatenate([b_p4, b_m4], 0))],
    )
    b_out = jnp.where(active_rows[:, None], b_total, 0.0).astype(jnp.bfloat16)
    low_all = placed(low_all, low_o, 2)
    a_total = product(
        ADAPTER_SCALE * contract(adapter_backward, adapter_down_factors[:a_width], 1, 1),
        [(i, low_all[i]) for i in range(4)],
    )
    high_all = placed(spread(high), high_m, 3)

    high_p, high_o, high_all, b_out, a_total = together(high_p, high_o, high_all, b_out, a_total)
    high_all = placed(placed(high_all, high_p, 1), high_o, 2)
    head_feature_gradient = in_vmem(
        last_kernel,
        head_outputs.shape,
        jnp.bfloat16,
        by_z,
        high_all.reshape(NZ // 2, by_z.shape[2], a_width),
        a_total,
        live,
        b_out,
    )
    return (head_feature_gradient, down_factor_gradient, up_factor_gradient)


def solution(mesh):
    in_specs = (
        P("dp", "tensor"),
        P(("dp", "tensor"), None),
        P("dp", "tensor"),
        P("tensor", "dp"),
        P("dp", None),
        P("dp"),
        P("dp"),
    )
    out_specs = (P("dp", "tensor"), P("tensor", "dp"), P("dp", None))
    return jax.shard_map(body, mesh=mesh, in_specs=in_specs, out_specs=out_specs, check_vma=False)
```

```python
import jax
import jax.numpy as jnp
from jax import lax
from jax.experimental import pallas as pl
from jax.experimental.pallas import tpu as pltpu
from jax.sharding import PartitionSpec as P

ADAPTER_RANK = 16
TEN_DEV = 8
ADAPTER_SCALE = 2.0
NZ, NX, NY = 8, 2, 4


def contract(left, right, left_dim, right_dim):
    return lax.dot_general(
        left, right, (((left_dim,), (right_dim,)), ((), ())), preferred_element_type=jnp.float32
    )


def fetch(x, dz=0, dx=0, dy=0):
    pairs = []
    for z in range(NZ):
        for a in range(NX):
            for y in range(NY):
                source = (((z + dz) % NZ) * NX + (a + dx) % NX) * NY + (y + dy) % NY
                pairs.append((source, (z * NX + a) * NY + y))
    return lax.ppermute(x, "dp", pairs)


def swap_tensor(x, mask):
    return lax.ppermute(x, "tensor", [(t, t ^ mask) for t in range(4)])


def together(*values):
    return lax.optimization_barrier(values)


def split_kernel(start_ref, g_ref, z_ref):
    width = z_ref.shape[2]
    for block in range(NZ):
        slot = lax.rem(block - start_ref[0] + NZ, NZ)
        z_ref[slot] = g_ref[:, block * width : (block + 1) * width]


def split_columns(gradients, start):
    rows, depth = gradients.shape
    step = rows // 4
    width = depth // NZ
    return pl.pallas_call(
        split_kernel,
        grid_spec=pltpu.PrefetchScalarGridSpec(
            num_scalar_prefetch=1,
            grid=(4,),
            in_specs=[pl.BlockSpec((step, depth), lambda i, s: (i, 0))],
            out_specs=pl.BlockSpec((NZ, step, width), lambda i, s: (0, i, 0)),
        ),
        out_shape=jax.ShapeDtypeStruct((NZ, rows, width), gradients.dtype),
        compiler_params=pltpu.CompilerParams(vmem_limit_bytes=32 * 1024 * 1024),
    )(start, gradients)


def last_kernel(z_ref, w_ref, total_ref, live_ref, b_ref, out_ref):
    width = w_ref.shape[2]
    count = w_ref.shape[0]
    total = total_ref[...]
    for i in range(count):
        total += contract(z_ref[NZ - count + i], w_ref[i], 1, 0)
    out_ref[:, :width] = jnp.where(live_ref[...] > 0, total, 0.0).astype(out_ref.dtype)
    out_ref[:, width:] = b_ref[...]


def down_kernel(head_ref, back_ref, out_ref):
    out_ref[...] = ADAPTER_SCALE * contract(head_ref[...], back_ref[...], 0, 0)


def in_vmem(kernel, shape, dtype, *arrays):
    return pl.pallas_call(
        kernel,
        in_specs=[pl.BlockSpec(memory_space=pltpu.VMEM)] * len(arrays),
        out_specs=pl.BlockSpec(memory_space=pltpu.VMEM),
        out_shape=jax.ShapeDtypeStruct(shape, dtype),
        compiler_params=pltpu.CompilerParams(vmem_limit_bytes=40 * 1024 * 1024),
    )(*arrays)


def body(
    head_outputs,
    output_gradient,
    frozen_weight,
    adapter_down_factors,
    adapter_up_factors,
    tenant_index,
    tenant_group_counts,
):
    row_count = head_outputs.shape[0]
    part_rows, depth = output_gradient.shape
    shard_rows, feature_width = frozen_weight.shape
    a_width = feature_width * 5 // 8
    group = lax.axis_index("dp").astype(jnp.int32)
    z, xl, y = group // (NX * NY), (group // NY) % NX, group % NY
    tensor = lax.axis_index("tensor").astype(jnp.int32)
    zero = jnp.int32(0)

    other = fetch(frozen_weight, dx=1)
    from_core = swap_tensor(output_gradient, 1)
    partial = jnp.dot(head_outputs, adapter_down_factors, preferred_element_type=jnp.float32)
    core_partial = swap_tensor(partial, 1)
    other, from_core, own_rows, index_later = together(
        other, from_core, output_gradient, tenant_index
    )

    def pair(columns):
        mine, far = frozen_weight[:, columns], other[:, columns]
        return jnp.where(xl == 0, jnp.stack([mine, far]), jnp.stack([far, mine]))

    pair_a, pair_b, own_rows = together(
        pair(slice(0, a_width)), pair(slice(a_width, None)), own_rows
    )
    a_p1, a_m1 = fetch(pair_a, dz=1), fetch(pair_a, dz=-1)
    y_b = [fetch(pair_b, dy=dy) for dy in (1, 2, 3)]
    from_chip = swap_tensor(own_rows, 2)

    a_p1, a_m1, pair_a, core_partial = together(a_p1, a_m1, pair_a, core_partial)
    a_p2, a_m2 = fetch(a_p1, dz=1), fetch(a_m1, dz=-1)
    a_p4 = fetch(pair_a, dz=4)

    def placed(array, chunk, dy):
        at = array.ndim - 3
        return lax.dynamic_update_slice_in_dim(
            array, jnp.expand_dims(chunk, at), (y + dy) % NY, at
        )

    def spread(chunk):
        at = chunk.ndim - 2
        shape = chunk.shape[:at] + (NY,) + chunk.shape[at:]
        return jnp.broadcast_to(jnp.expand_dims(chunk, at), shape)

    *y_b, pair_b, a_p1 = together(*y_b, pair_b, a_p1)
    b_own = spread(pair_b)
    for dy, chunk in zip((1, 2, 3), y_b):
        b_own = placed(b_own, chunk, dy)
    b_own = b_own.reshape(NX * NY * shard_rows, -1)

    a_p2, a_m2, b_own = together(a_p2, a_m2, b_own)
    low = jnp.stack([a_m1, pair_a, a_p1, a_p2])
    low_p, low_m = fetch(low, dy=1), fetch(low, dy=-1)
    a_p3, a_m3 = fetch(a_p2, dz=1), fetch(a_m2, dz=-1)
    b_p1, b_m1 = fetch(b_own, dz=1), fetch(b_own, dz=-1)
    high = jnp.stack([a_p3, a_p4, a_m3, a_m2])

    b_p1, b_m1, low_p, low_m, high, from_chip, own_rows, partial, core_partial = together(
        b_p1, b_m1, low_p, low_m, high, from_chip, own_rows, partial, core_partial
    )
    b_p2, b_m2 = fetch(b_p1, dz=1), fetch(b_m1, dz=-1)
    low_o, high_m = fetch(low_p, dy=1), fetch(high, dy=-1)

    from_both = swap_tensor(from_chip, 1)
    gradients = jnp.zeros((row_count, depth), output_gradient.dtype)
    for block, mask in ((own_rows, 0), (from_core, 1), (from_chip, 2), (from_both, 3)):
        gradients = lax.dynamic_update_slice_in_dim(
            gradients, block, (tensor ^ mask) * part_rows, 0
        )

    from_both, partial, core_partial = together(from_both, partial, core_partial)
    chip_sum = partial + core_partial
    far_sum = swap_tensor(chip_sum, 2)
    low_all = placed(placed(spread(low), low_p, 1), low_m, 3)

    b_p2, b_m2, gradients = together(b_p2, b_m2, gradients)
    b_p3, b_m3 = fetch(b_p2, dz=1), fetch(b_m2, dz=-1)
    low_o, high_m, high, low_all, b_p2 = together(low_o, high_m, high, low_all, b_p2)
    high_p, high_o = fetch(high, dy=1), fetch(high_m, dy=-1)
    by_z = split_columns(gradients, ((z + NZ - 1) % NZ).reshape(1))

    position = jnp.arange(row_count, dtype=jnp.int32)
    active_rows = position < tenant_group_counts[0]
    slot_lookup = jnp.arange(adapter_down_factors.shape[1], dtype=jnp.int32) // ADAPTER_RANK
    select_rows = (
        active_rows[:, None] & (slot_lookup[None, :] == (index_later % TEN_DEV)[:, None])
    ).astype(jnp.float32)
    adapter_backward = (contract(gradients, adapter_up_factors, 1, 1) * select_rows).astype(
        jnp.bfloat16
    )
    down_factor_gradient = in_vmem(
        down_kernel, adapter_down_factors.shape, jnp.float32, head_outputs, adapter_backward
    )
    live = active_rows.astype(jnp.float32)[:, None]

    b_p3, b_m3, by_z, adapter_backward, down_factor_gradient = together(
        b_p3, b_m3, by_z, adapter_backward, down_factor_gradient
    )
    cut = b_own.shape[0] // 2 // 16 * 16
    b_p4, b_m4 = fetch(b_p3[:cut], dz=1), fetch(b_m3[cut:], dz=-1)
    adapter_input = ((chip_sum + far_sum) * select_rows).astype(jnp.bfloat16)
    (adapter_input,) = together(adapter_input)
    up_factor_gradient = ADAPTER_SCALE * contract(adapter_input, gradients, 0, 0)

    def product(total, terms):
        for slot, chunk in terms:
            total = total + contract(by_z[slot], chunk.reshape(by_z.shape[2], -1), 1, 0)
        return total

    b_p4, b_m4, up_factor_gradient, low_all, high_m = together(
        b_p4, b_m4, up_factor_gradient, low_all, high_m
    )
    b_total = product(
        ADAPTER_SCALE * contract(adapter_backward, adapter_down_factors[a_width:], 1, 1),
        [(1, b_own), (0, b_m1), (2, b_p1), (7, b_m2), (3, b_p2), (6, b_m3), (4, b_p3)]
        + [(5, jnp.concatenate([b_p4, b_m4], 0))],
    )
    b_out = jnp.where(active_rows[:, None], b_total, 0.0).astype(jnp.bfloat16)
    low_all = placed(low_all, low_o, 2)
    a_total = product(
        ADAPTER_SCALE * contract(adapter_backward, adapter_down_factors[:a_width], 1, 1),
        [(i, low_all[i]) for i in range(4)],
    )
    high_all = placed(spread(high), high_m, 3)

    high_p, high_o, high_all, b_out, a_total = together(high_p, high_o, high_all, b_out, a_total)
    high_all = placed(placed(high_all, high_p, 1), high_o, 2)
    head_feature_gradient = in_vmem(
        last_kernel,
        head_outputs.shape,
        jnp.bfloat16,
        by_z,
        high_all.reshape(NZ // 2, by_z.shape[2], a_width),
        a_total,
        live,
        b_out,
    )
    return (head_feature_gradient, down_factor_gradient, up_factor_gradient)


def solution(mesh):
    in_specs = (
        P("dp", "tensor"),
        P(("dp", "tensor"), None),
        P("dp", "tensor"),
        P("tensor", "dp"),
        P("dp", None),
        P("dp"),
        P("dp"),
    )
    out_specs = (P("dp", "tensor"), P("tensor", "dp"), P("dp", None))
    return jax.shard_map(body, mesh=mesh, in_specs=in_specs, out_specs=out_specs, check_vma=False)
```

```python
import jax
import jax.numpy as jnp
from jax import lax
from jax.experimental import pallas as pl
from jax.experimental.pallas import tpu as pltpu
from jax.sharding import PartitionSpec as P

ADAPTER_RANK = 16
TEN_DEV = 8
ADAPTER_SCALE = 2.0
NZ, NX, NY = 8, 2, 4


def contract(left, right, left_dim, right_dim):
    return lax.dot_general(
        left, right, (((left_dim,), (right_dim,)), ((), ())), preferred_element_type=jnp.float32
    )


def fetch(x, dz=0, dx=0, dy=0):
    pairs = []
    for z in range(NZ):
        for a in range(NX):
            for y in range(NY):
                source = (((z + dz) % NZ) * NX + (a + dx) % NX) * NY + (y + dy) % NY
                pairs.append((source, (z * NX + a) * NY + y))
    return lax.ppermute(x, "dp", pairs)


def swap_tensor(x, mask):
    return lax.ppermute(x, "tensor", [(t, t ^ mask) for t in range(4)])


def together(*values):
    return lax.optimization_barrier(values)


def split_kernel(start_ref, g_ref, z_ref):
    width = z_ref.shape[2]
    for block in range(NZ):
        slot = lax.rem(block - start_ref[0] + NZ, NZ)
        z_ref[slot] = g_ref[:, block * width : (block + 1) * width]


def split_columns(gradients, start):
    rows, depth = gradients.shape
    step = rows // 4
    width = depth // NZ
    return pl.pallas_call(
        split_kernel,
        grid_spec=pltpu.PrefetchScalarGridSpec(
            num_scalar_prefetch=1,
            grid=(4,),
            in_specs=[pl.BlockSpec((step, depth), lambda i, s: (i, 0))],
            out_specs=pl.BlockSpec((NZ, step, width), lambda i, s: (0, i, 0)),
        ),
        out_shape=jax.ShapeDtypeStruct((NZ, rows, width), gradients.dtype),
        compiler_params=pltpu.CompilerParams(vmem_limit_bytes=32 * 1024 * 1024),
    )(start, gradients)


def last_kernel(z_ref, w_ref, total_ref, live_ref, b_ref, out_ref):
    width = w_ref.shape[2]
    count = w_ref.shape[0]
    total = total_ref[...]
    for i in range(count):
        total += contract(z_ref[NZ - count + i], w_ref[i], 1, 0)
    out_ref[:, :width] = jnp.where(live_ref[...] > 0, total, 0.0).astype(out_ref.dtype)
    out_ref[:, width:] = b_ref[...]


def down_kernel(head_ref, back_ref, out_ref):
    out_ref[...] = ADAPTER_SCALE * contract(head_ref[...], back_ref[...], 0, 0)


def in_vmem(kernel, shape, dtype, *arrays):
    return pl.pallas_call(
        kernel,
        in_specs=[pl.BlockSpec(memory_space=pltpu.VMEM)] * len(arrays),
        out_specs=pl.BlockSpec(memory_space=pltpu.VMEM),
        out_shape=jax.ShapeDtypeStruct(shape, dtype),
        compiler_params=pltpu.CompilerParams(vmem_limit_bytes=40 * 1024 * 1024),
    )(*arrays)


def body(
    head_outputs,
    output_gradient,
    frozen_weight,
    adapter_down_factors,
    adapter_up_factors,
    tenant_index,
    tenant_group_counts,
):
    row_count = head_outputs.shape[0]
    part_rows, depth = output_gradient.shape
    shard_rows, feature_width = frozen_weight.shape
    a_width = feature_width * 5 // 8
    group = lax.axis_index("dp").astype(jnp.int32)
    z, xl, y = group // (NX * NY), (group // NY) % NX, group % NY
    tensor = lax.axis_index("tensor").astype(jnp.int32)
    zero = jnp.int32(0)

    other = fetch(frozen_weight, dx=1)
    from_core = swap_tensor(output_gradient, 1)
    partial = jnp.dot(head_outputs, adapter_down_factors, preferred_element_type=jnp.float32)
    core_partial = swap_tensor(partial, 1)
    partial, own_rows = together(partial, output_gradient)
    from_chip = swap_tensor(own_rows, 2)
    other, from_core, index_later = together(other, from_core, tenant_index)

    def pair(columns):
        mine, far = frozen_weight[:, columns], other[:, columns]
        return jnp.where(xl == 0, jnp.stack([mine, far]), jnp.stack([far, mine]))

    pair_a = pair(slice(0, a_width))
    pair_b = pair(slice(a_width, None))
    a_p1, a_m1 = fetch(pair_a, dz=1), fetch(pair_a, dz=-1)
    y_b1, y_b3 = fetch(pair_b, dy=1), fetch(pair_b, dy=-1)

    a_p1, a_m1, pair_a, pair_b, core_partial = together(a_p1, a_m1, pair_a, pair_b, core_partial)
    a_p2, a_m2 = fetch(a_p1, dz=1), fetch(a_m1, dz=-1)
    y_b = [y_b1, fetch(pair_b, dy=2), y_b3]

    def placed(array, chunk, dy):
        at = array.ndim - 3
        return lax.dynamic_update_slice_in_dim(
            array, jnp.expand_dims(chunk, at), (y + dy) % NY, at
        )

    def spread(chunk):
        at = chunk.ndim - 2
        shape = chunk.shape[:at] + (NY,) + chunk.shape[at:]
        return jnp.broadcast_to(jnp.expand_dims(chunk, at), shape)

    a_p2, a_m2, pair_b, *y_b = together(a_p2, a_m2, pair_b, *y_b)
    low = jnp.stack([a_m1, pair_a, a_p1, a_p2])
    low_p, low_m = fetch(low, dy=1), fetch(low, dy=-1)
    a_p3, a_m3 = fetch(a_p2, dz=1), fetch(a_m2, dz=-1)
    b_own = spread(pair_b)
    for dy, chunk in zip((1, 2, 3), y_b):
        b_own = placed(b_own, chunk, dy)
    b_own = b_own.reshape(NX * NY * shard_rows, -1)

    a_p3, a_m3, b_own, from_chip = together(a_p3, a_m3, b_own, from_chip)
    a_p4 = fetch(a_p3, dz=1)
    b_p1, b_m1 = fetch(b_own, dz=1), fetch(b_own, dz=-1)
    high = jnp.stack([a_p3, a_p4, a_m3, a_m2])

    low_p, low_m, high = together(low_p, low_m, high)
    low_o, high_m = fetch(low_p, dy=1), fetch(high, dy=-1)
    b_p1, b_m1, low_p = together(b_p1, b_m1, low_p)
    b_p2, b_m2 = fetch(b_p1, dz=1), fetch(b_m1, dz=-1)

    from_both = swap_tensor(from_chip, 1)
    gradients = jnp.zeros((row_count, depth), output_gradient.dtype)
    for block, mask in ((own_rows, 0), (from_core, 1), (from_chip, 2), (from_both, 3)):
        gradients = lax.dynamic_update_slice_in_dim(
            gradients, block, (tensor ^ mask) * part_rows, 0
        )

    from_both, partial, core_partial = together(from_both, partial, core_partial)
    chip_sum = partial + core_partial
    far_sum = swap_tensor(chip_sum, 2)
    low_all = placed(placed(spread(low), low_p, 1), low_m, 3)

    by_z = split_columns(gradients, ((z + NZ - 1) % NZ).reshape(1))

    position = jnp.arange(row_count, dtype=jnp.int32)
    active_rows = position < tenant_group_counts[0]
    slot_lookup = jnp.arange(adapter_down_factors.shape[1], dtype=jnp.int32) // ADAPTER_RANK
    select_rows = (
        active_rows[:, None] & (slot_lookup[None, :] == (index_later % TEN_DEV)[:, None])
    ).astype(jnp.float32)
    adapter_backward = (contract(gradients, adapter_up_factors, 1, 1) * select_rows).astype(
        jnp.bfloat16
    )
    down_factor_gradient = in_vmem(
        down_kernel, adapter_down_factors.shape, jnp.float32, head_outputs, adapter_backward
    )
    live = active_rows.astype(jnp.float32)[:, None]

    def product(total, terms):
        for slot, chunk in terms:
            total = total + contract(by_z[slot], chunk.reshape(by_z.shape[2], -1), 1, 0)
        return total

    b_total = product(
        ADAPTER_SCALE * contract(adapter_backward, adapter_down_factors[a_width:], 1, 1),
        [(1, b_own), (0, b_m1), (2, b_p1)],
    )

    (
        b_p2, b_m2, low_o, high_m, high, low_all, far_sum, by_z, adapter_backward,
        down_factor_gradient, b_total,
    ) = together(
        b_p2, b_m2, low_o, high_m, high, low_all, far_sum, by_z, adapter_backward,
        down_factor_gradient, b_total,
    )
    high_p, high_o = fetch(high, dy=1), fetch(high_m, dy=-1)
    b_p3, b_m3 = fetch(b_p2, dz=1), fetch(b_m2, dz=-1)
    b_p3, b_m3 = together(b_p3, b_m3)
    cut = b_own.shape[0] // 2 // 16 * 16
    b_p4, b_m4 = fetch(b_p3[:cut], dz=1), fetch(b_m3[cut:], dz=-1)
    adapter_input = ((chip_sum + far_sum) * select_rows).astype(jnp.bfloat16)
    (adapter_input,) = together(adapter_input)
    up_factor_gradient = ADAPTER_SCALE * contract(adapter_input, gradients, 0, 0)

    b_p4, b_m4, up_factor_gradient, low_all, high_m = together(
        b_p4, b_m4, up_factor_gradient, low_all, high_m
    )
    b_total = product(
        b_total,
        [(7, b_m2), (3, b_p2), (6, b_m3), (4, b_p3), (5, jnp.concatenate([b_p4, b_m4], 0))],
    )
    b_out = jnp.where(active_rows[:, None], b_total, 0.0).astype(jnp.bfloat16)
    low_all = placed(low_all, low_o, 2)
    a_total = product(
        ADAPTER_SCALE * contract(adapter_backward, adapter_down_factors[:a_width], 1, 1),
        [(i, low_all[i]) for i in range(4)],
    )
    high_all = placed(spread(high), high_m, 3)

    high_p, high_o, high_all, b_out, a_total = together(high_p, high_o, high_all, b_out, a_total)
    high_all = placed(placed(high_all, high_p, 1), high_o, 2)
    head_feature_gradient = in_vmem(
        last_kernel,
        head_outputs.shape,
        jnp.bfloat16,
        by_z,
        high_all.reshape(NZ // 2, by_z.shape[2], a_width),
        a_total,
        live,
        b_out,
    )
    return (head_feature_gradient, down_factor_gradient, up_factor_gradient)


def solution(mesh):
    in_specs = (
        P("dp", "tensor"),
        P(("dp", "tensor"), None),
        P("dp", "tensor"),
        P("tensor", "dp"),
        P("dp", None),
        P("dp"),
        P("dp"),
    )
    out_specs = (P("dp", "tensor"), P("tensor", "dp"), P("dp", None))
    return jax.shard_map(body, mesh=mesh, in_specs=in_specs, out_specs=out_specs, check_vma=False)
```

```python
import jax
import jax.numpy as jnp
from jax import lax
from jax.experimental import pallas as pl
from jax.experimental.pallas import tpu as pltpu
from jax.sharding import PartitionSpec as P

ADAPTER_RANK = 16
TEN_DEV = 8
ADAPTER_SCALE = 2.0
NZ, NX, NY = 8, 2, 4


def contract(left, right, left_dim, right_dim):
    return lax.dot_general(
        left, right, (((left_dim,), (right_dim,)), ((), ())), preferred_element_type=jnp.float32
    )


def fetch(x, dz=0, dx=0, dy=0):
    pairs = []
    for z in range(NZ):
        for a in range(NX):
            for y in range(NY):
                source = (((z + dz) % NZ) * NX + (a + dx) % NX) * NY + (y + dy) % NY
                pairs.append((source, (z * NX + a) * NY + y))
    return lax.ppermute(x, "dp", pairs)


def swap_tensor(x, mask):
    return lax.ppermute(x, "tensor", [(t, t ^ mask) for t in range(4)])


def together(*values):
    return lax.optimization_barrier(values)


def split_kernel(start_ref, g_ref, z_ref):
    width = z_ref.shape[2]
    for block in range(NZ):
        slot = lax.rem(block - start_ref[0] + NZ, NZ)
        z_ref[slot] = g_ref[:, block * width : (block + 1) * width]


def split_columns(gradients, start):
    rows, depth = gradients.shape
    step = rows // 4
    width = depth // NZ
    return pl.pallas_call(
        split_kernel,
        grid_spec=pltpu.PrefetchScalarGridSpec(
            num_scalar_prefetch=1,
            grid=(4,),
            in_specs=[pl.BlockSpec((step, depth), lambda i, s: (i, 0))],
            out_specs=pl.BlockSpec((NZ, step, width), lambda i, s: (0, i, 0)),
        ),
        out_shape=jax.ShapeDtypeStruct((NZ, rows, width), gradients.dtype),
        compiler_params=pltpu.CompilerParams(vmem_limit_bytes=32 * 1024 * 1024),
    )(start, gradients)


def last_kernel(z_ref, w_ref, total_ref, live_ref, b_ref, out_ref):
    width = w_ref.shape[2]
    count = w_ref.shape[0]
    total = total_ref[...]
    for i in range(count):
        total += contract(z_ref[NZ - count + i], w_ref[i], 1, 0)
    out_ref[:, :width] = jnp.where(live_ref[...] > 0, total, 0.0).astype(out_ref.dtype)
    out_ref[:, width:] = b_ref[...]


def pair_kernel(x_ref, mine_ref, far_ref, a_ref, b_ref):
    width = a_ref.shape[2]
    x = x_ref[0]
    for slot, ref in ((x, mine_ref), (1 - x, far_ref)):
        a_ref[slot] = ref[:, :width]
        b_ref[slot] = ref[:, width:]


def pairs(x, mine, far, a_width):
    rows, width = mine.shape
    shapes = [(NX, rows, a_width), (NX, rows, width - a_width)]
    vmem = pl.BlockSpec(memory_space=pltpu.VMEM)
    return pl.pallas_call(
        pair_kernel,
        in_specs=[pl.BlockSpec(memory_space=pltpu.SMEM), vmem, vmem],
        out_specs=[vmem, vmem],
        out_shape=[jax.ShapeDtypeStruct(shape, mine.dtype) for shape in shapes],
    )(x, mine, far)


def down_kernel(head_ref, back_ref, out_ref):
    out_ref[...] = ADAPTER_SCALE * contract(head_ref[...], back_ref[...], 0, 0)


def in_vmem(kernel, shape, dtype, *arrays):
    return pl.pallas_call(
        kernel,
        in_specs=[pl.BlockSpec(memory_space=pltpu.VMEM)] * len(arrays),
        out_specs=pl.BlockSpec(memory_space=pltpu.VMEM),
        out_shape=jax.ShapeDtypeStruct(shape, dtype),
        compiler_params=pltpu.CompilerParams(vmem_limit_bytes=40 * 1024 * 1024),
    )(*arrays)


def body(
    head_outputs,
    output_gradient,
    frozen_weight,
    adapter_down_factors,
    adapter_up_factors,
    tenant_index,
    tenant_group_counts,
):
    row_count = head_outputs.shape[0]
    part_rows, depth = output_gradient.shape
    shard_rows, feature_width = frozen_weight.shape
    a_width = feature_width * 5 // 8
    group = lax.axis_index("dp").astype(jnp.int32)
    z, xl, y = group // (NX * NY), (group // NY) % NX, group % NY
    tensor = lax.axis_index("tensor").astype(jnp.int32)
    zero = jnp.int32(0)

    other = fetch(frozen_weight, dx=1)
    from_core = swap_tensor(output_gradient, 1)
    partial = jnp.dot(head_outputs, adapter_down_factors, preferred_element_type=jnp.float32)
    core_partial = swap_tensor(partial, 1)
    partial, own_rows = together(partial, output_gradient)
    from_chip = swap_tensor(own_rows, 2)
    other, from_core, index_later = together(other, from_core, tenant_index)

    pair_a, pair_b = pairs(xl.reshape(1), frozen_weight, other, a_width)
    a_p1, a_m1 = fetch(pair_a, dz=1), fetch(pair_a, dz=-1)
    y_b1, y_b3 = fetch(pair_b, dy=1), fetch(pair_b, dy=-1)

    a_p1, a_m1, pair_a, pair_b, core_partial = together(a_p1, a_m1, pair_a, pair_b, core_partial)
    a_p2, a_m2 = fetch(a_p1, dz=1), fetch(a_m1, dz=-1)
    y_b = [y_b1, fetch(pair_b, dy=2), y_b3]

    def placed(array, chunk, dy):
        at = array.ndim - 3
        return lax.dynamic_update_slice_in_dim(
            array, jnp.expand_dims(chunk, at), (y + dy) % NY, at
        )

    def spread(chunk):
        at = chunk.ndim - 2
        shape = chunk.shape[:at] + (NY,) + chunk.shape[at:]
        return jnp.broadcast_to(jnp.expand_dims(chunk, at), shape)

    a_p2, a_m2, pair_b, *y_b = together(a_p2, a_m2, pair_b, *y_b)
    low = jnp.stack([a_m1, pair_a, a_p1, a_p2])
    low_p, low_m = fetch(low, dy=1), fetch(low, dy=-1)
    a_p3, a_m3 = fetch(a_p2, dz=1), fetch(a_m2, dz=-1)
    b_own = spread(pair_b)
    for dy, chunk in zip((1, 2, 3), y_b):
        b_own = placed(b_own, chunk, dy)
    b_own = b_own.reshape(NX * NY * shard_rows, -1)

    a_p3, a_m3, b_own, from_chip, partial, core_partial = together(
        a_p3, a_m3, b_own, from_chip, partial, core_partial
    )
    chip_sum = partial + core_partial
    far_sum = swap_tensor(chip_sum, 2)
    a_p4 = fetch(a_p3, dz=1)
    b_p1, b_m1 = fetch(b_own, dz=1), fetch(b_own, dz=-1)
    high = jnp.stack([a_p3, a_p4, a_m3, a_m2])

    low_p, low_m, high = together(low_p, low_m, high)
    low_o, high_m = fetch(low_p, dy=1), fetch(high, dy=-1)
    b_p1, b_m1, low_p, far_sum, own_rows, from_core = together(
        b_p1, b_m1, low_p, far_sum, own_rows, from_core
    )
    b_p2, b_m2 = fetch(b_p1, dz=1), fetch(b_m1, dz=-1)

    from_both = swap_tensor(from_chip, 1)
    gradients = jnp.zeros((row_count, depth), output_gradient.dtype)
    for block, mask in ((own_rows, 0), (from_core, 1), (from_chip, 2), (from_both, 3)):
        gradients = lax.dynamic_update_slice_in_dim(
            gradients, block, (tensor ^ mask) * part_rows, 0
        )

    low_all = placed(placed(spread(low), low_p, 1), low_m, 3)

    by_z = split_columns(gradients, ((z + NZ - 1) % NZ).reshape(1))

    position = jnp.arange(row_count, dtype=jnp.int32)
    active_rows = position < tenant_group_counts[0]
    slot_lookup = jnp.arange(adapter_down_factors.shape[1], dtype=jnp.int32) // ADAPTER_RANK
    select_rows = (
        active_rows[:, None] & (slot_lookup[None, :] == (index_later % TEN_DEV)[:, None])
    ).astype(jnp.float32)
    adapter_backward = (contract(gradients, adapter_up_factors, 1, 1) * select_rows).astype(
        jnp.bfloat16
    )
    down_factor_gradient = in_vmem(
        down_kernel, adapter_down_factors.shape, jnp.float32, head_outputs, adapter_backward
    )
    live = active_rows.astype(jnp.float32)[:, None]

    def product(total, terms):
        for slot, chunk in terms:
            total = total + contract(by_z[slot], chunk.reshape(by_z.shape[2], -1), 1, 0)
        return total

    b_total = product(
        ADAPTER_SCALE * contract(adapter_backward, adapter_down_factors[a_width:], 1, 1),
        [(1, b_own), (0, b_m1), (2, b_p1)],
    )

    (
        b_p2, b_m2, low_o, high_m, high, low_all, by_z, adapter_backward,
        down_factor_gradient, b_total,
    ) = together(
        b_p2, b_m2, low_o, high_m, high, low_all, by_z, adapter_backward,
        down_factor_gradient, b_total,
    )
    high_p, high_o = fetch(high, dy=1), fetch(high_m, dy=-1)
    b_p3, b_m3 = fetch(b_p2, dz=1), fetch(b_m2, dz=-1)
    b_p3, b_m3 = together(b_p3, b_m3)
    cut = b_own.shape[0] // 2 // 16 * 16
    b_p4, b_m4 = fetch(b_p3[:cut], dz=1), fetch(b_m3[cut:], dz=-1)
    adapter_input = ((chip_sum + far_sum) * select_rows).astype(jnp.bfloat16)
    (adapter_input,) = together(adapter_input)
    up_factor_gradient = ADAPTER_SCALE * contract(adapter_input, gradients, 0, 0)

    b_p4, b_m4, up_factor_gradient, low_all, high_m = together(
        b_p4, b_m4, up_factor_gradient, low_all, high_m
    )
    b_total = product(
        b_total,
        [(7, b_m2), (3, b_p2), (6, b_m3), (4, b_p3), (5, jnp.concatenate([b_p4, b_m4], 0))],
    )
    b_out = jnp.where(active_rows[:, None], b_total, 0.0).astype(jnp.bfloat16)
    low_all = placed(low_all, low_o, 2)
    a_total = product(
        ADAPTER_SCALE * contract(adapter_backward, adapter_down_factors[:a_width], 1, 1),
        [(i, low_all[i]) for i in range(4)],
    )
    high_all = placed(spread(high), high_m, 3)

    high_p, high_o, high_all, b_out, a_total = together(high_p, high_o, high_all, b_out, a_total)
    high_all = placed(placed(high_all, high_p, 1), high_o, 2)
    head_feature_gradient = in_vmem(
        last_kernel,
        head_outputs.shape,
        jnp.bfloat16,
        by_z,
        high_all.reshape(NZ // 2, by_z.shape[2], a_width),
        a_total,
        live,
        b_out,
    )
    return (head_feature_gradient, down_factor_gradient, up_factor_gradient)


def solution(mesh):
    in_specs = (
        P("dp", "tensor"),
        P(("dp", "tensor"), None),
        P("dp", "tensor"),
        P("tensor", "dp"),
        P("dp", None),
        P("dp"),
        P("dp"),
    )
    out_specs = (P("dp", "tensor"), P("tensor", "dp"), P("dp", None))
    return jax.shard_map(body, mesh=mesh, in_specs=in_specs, out_specs=out_specs, check_vma=False)
```

```python
import jax
import jax.numpy as jnp
from jax import lax
from jax.experimental import pallas as pl
from jax.experimental.pallas import tpu as pltpu
from jax.sharding import PartitionSpec as P

ADAPTER_RANK = 16
TEN_DEV = 8
ADAPTER_SCALE = 2.0
NZ, NX, NY = 8, 2, 4


def contract(left, right, left_dim, right_dim):
    return lax.dot_general(
        left, right, (((left_dim,), (right_dim,)), ((), ())), preferred_element_type=jnp.float32
    )


def fetch(x, dz=0, dx=0, dy=0):
    pairs = []
    for z in range(NZ):
        for a in range(NX):
            for y in range(NY):
                source = (((z + dz) % NZ) * NX + (a + dx) % NX) * NY + (y + dy) % NY
                pairs.append((source, (z * NX + a) * NY + y))
    return lax.ppermute(x, "dp", pairs)


def swap_tensor(x, mask):
    return lax.ppermute(x, "tensor", [(t, t ^ mask) for t in range(4)])


def together(*values):
    return lax.optimization_barrier(values)


def split_kernel(start_ref, g_ref, z_ref):
    width = z_ref.shape[2]
    for block in range(NZ):
        slot = lax.rem(block - start_ref[0] + NZ, NZ)
        z_ref[slot] = g_ref[:, block * width : (block + 1) * width]


def split_columns(gradients, start):
    rows, depth = gradients.shape
    step = rows // 4
    width = depth // NZ
    return pl.pallas_call(
        split_kernel,
        grid_spec=pltpu.PrefetchScalarGridSpec(
            num_scalar_prefetch=1,
            grid=(4,),
            in_specs=[pl.BlockSpec((step, depth), lambda i, s: (i, 0))],
            out_specs=pl.BlockSpec((NZ, step, width), lambda i, s: (0, i, 0)),
        ),
        out_shape=jax.ShapeDtypeStruct((NZ, rows, width), gradients.dtype),
        compiler_params=pltpu.CompilerParams(vmem_limit_bytes=32 * 1024 * 1024),
    )(start, gradients)


def last_kernel(z_ref, w_ref, total_ref, live_ref, b_ref, out_ref):
    width = w_ref.shape[2]
    count = w_ref.shape[0]
    total = total_ref[...]
    for i in range(count):
        total += contract(z_ref[NZ - count + i], w_ref[i], 1, 0)
    out_ref[:, :width] = jnp.where(live_ref[...] > 0, total, 0.0).astype(out_ref.dtype)
    out_ref[:, width:] = b_ref[...]


def pair_kernel(x_ref, mine_ref, far_ref, a_ref, b_ref):
    width = a_ref.shape[2]
    x = x_ref[0]
    for slot, ref in ((x, mine_ref), (1 - x, far_ref)):
        a_ref[slot] = ref[:, :width]
        b_ref[slot] = ref[:, width:]


def pairs(x, mine, far, a_width):
    rows, width = mine.shape
    shapes = [(NX, rows, a_width), (NX, rows, width - a_width)]
    vmem = pl.BlockSpec(memory_space=pltpu.VMEM)
    return pl.pallas_call(
        pair_kernel,
        in_specs=[pl.BlockSpec(memory_space=pltpu.SMEM), vmem, vmem],
        out_specs=[vmem, vmem],
        out_shape=[jax.ShapeDtypeStruct(shape, mine.dtype) for shape in shapes],
    )(x, mine, far)


def down_kernel(head_ref, back_ref, out_ref):
    out_ref[...] = ADAPTER_SCALE * contract(head_ref[...], back_ref[...], 0, 0)


def in_vmem(kernel, shape, dtype, *arrays):
    return pl.pallas_call(
        kernel,
        in_specs=[pl.BlockSpec(memory_space=pltpu.VMEM)] * len(arrays),
        out_specs=pl.BlockSpec(memory_space=pltpu.VMEM),
        out_shape=jax.ShapeDtypeStruct(shape, dtype),
        compiler_params=pltpu.CompilerParams(vmem_limit_bytes=40 * 1024 * 1024),
    )(*arrays)


def body(
    head_outputs,
    output_gradient,
    frozen_weight,
    adapter_down_factors,
    adapter_up_factors,
    tenant_index,
    tenant_group_counts,
):
    row_count = head_outputs.shape[0]
    part_rows, depth = output_gradient.shape
    shard_rows, feature_width = frozen_weight.shape
    a_width = feature_width * 5 // 8
    group = lax.axis_index("dp").astype(jnp.int32)
    z, xl, y = group // (NX * NY), (group // NY) % NX, group % NY
    tensor = lax.axis_index("tensor").astype(jnp.int32)
    zero = jnp.int32(0)

    other = fetch(frozen_weight, dx=1)
    from_core = swap_tensor(output_gradient, 1)
    partial = jnp.dot(head_outputs, adapter_down_factors, preferred_element_type=jnp.float32)
    core_partial = swap_tensor(partial, 1)
    partial, own_rows = together(partial, output_gradient)
    from_chip = swap_tensor(own_rows, 2)
    other, from_core, index_later = together(other, from_core, tenant_index)

    pair_a, pair_b = pairs(xl.reshape(1), frozen_weight, other, a_width)
    a_p1, a_m1 = fetch(pair_a, dz=1), fetch(pair_a, dz=-1)
    y_b1, y_b3 = fetch(pair_b, dy=1), fetch(pair_b, dy=-1)

    a_p1, a_m1, pair_a, pair_b, core_partial = together(a_p1, a_m1, pair_a, pair_b, core_partial)
    a_p2, a_m2 = fetch(a_p1, dz=1), fetch(a_m1, dz=-1)
    y_b = [y_b1, fetch(pair_b, dy=2), y_b3]

    def placed(array, chunk, dy):
        at = array.ndim - 3
        return lax.dynamic_update_slice_in_dim(
            array, jnp.expand_dims(chunk, at), (y + dy) % NY, at
        )

    def spread(chunk):
        at = chunk.ndim - 2
        shape = chunk.shape[:at] + (NY,) + chunk.shape[at:]
        return jnp.broadcast_to(jnp.expand_dims(chunk, at), shape)

    a_p2, a_m2 = together(a_p2, a_m2)
    low = jnp.stack([a_m1, pair_a, a_p1, a_p2])
    low_p, low_m = fetch(low, dy=1), fetch(low, dy=-1)
    a_p3, a_m3 = fetch(a_p2, dz=1), fetch(a_m2, dz=-1)
    b_own = spread(pair_b)
    for dy, chunk in zip((1, 2, 3), y_b):
        b_own = placed(b_own, chunk, dy)
    b_own = b_own.reshape(NX * NY * shard_rows, -1)

    a_p3, a_m3, b_own = together(a_p3, a_m3, b_own)
    a_p4 = fetch(a_p3, dz=1)
    b_p1, b_m1 = fetch(b_own, dz=1), fetch(b_own, dz=-1)
    high = jnp.stack([a_p3, a_p4, a_m3, a_m2])

    low_p, low_m, high = together(low_p, low_m, high)
    low_o, high_m = fetch(low_p, dy=1), fetch(high, dy=-1)
    b_p1, b_m1, low_p, own_rows, from_core, from_chip = together(
        b_p1, b_m1, low_p, own_rows, from_core, from_chip
    )
    b_p2, b_m2 = fetch(b_p1, dz=1), fetch(b_m1, dz=-1)

    from_both = swap_tensor(from_chip, 1)
    gradients = jnp.zeros((row_count, depth), output_gradient.dtype)
    for block, mask in ((own_rows, 0), (from_core, 1), (from_chip, 2), (from_both, 3)):
        gradients = lax.dynamic_update_slice_in_dim(
            gradients, block, (tensor ^ mask) * part_rows, 0
        )

    low_all = placed(placed(spread(low), low_p, 1), low_m, 3)

    by_z = split_columns(gradients, ((z + NZ - 1) % NZ).reshape(1))

    position = jnp.arange(row_count, dtype=jnp.int32)
    active_rows = position < tenant_group_counts[0]
    slot_lookup = jnp.arange(adapter_down_factors.shape[1], dtype=jnp.int32) // ADAPTER_RANK
    select_rows = (
        active_rows[:, None] & (slot_lookup[None, :] == (index_later % TEN_DEV)[:, None])
    ).astype(jnp.float32)
    adapter_backward = (contract(gradients, adapter_up_factors, 1, 1) * select_rows).astype(
        jnp.bfloat16
    )
    down_factor_gradient = in_vmem(
        down_kernel, adapter_down_factors.shape, jnp.float32, head_outputs, adapter_backward
    )
    live = active_rows.astype(jnp.float32)[:, None]

    def product(total, terms):
        for slot, chunk in terms:
            total = total + contract(by_z[slot], chunk.reshape(by_z.shape[2], -1), 1, 0)
        return total

    b_total = product(
        ADAPTER_SCALE * contract(adapter_backward, adapter_down_factors[a_width:], 1, 1),
        [(1, b_own), (0, b_m1), (2, b_p1)],
    )

    (
        b_p2, b_m2, low_o, high_m, high, low_all, by_z, adapter_backward, partial,
        core_partial, down_factor_gradient, b_total,
    ) = together(
        b_p2, b_m2, low_o, high_m, high, low_all, by_z, adapter_backward, partial,
        core_partial, down_factor_gradient, b_total,
    )
    high_p, high_o = fetch(high, dy=1), fetch(high_m, dy=-1)
    b_p3, b_m3 = fetch(b_p2, dz=1), fetch(b_m2, dz=-1)
    chip_sum = partial + core_partial
    far_sum = swap_tensor(chip_sum, 2)
    low_all, low_o, far_sum, chip_sum = together(low_all, low_o, far_sum, chip_sum)
    low_all = placed(low_all, low_o, 2)
    a_total = product(
        ADAPTER_SCALE * contract(adapter_backward, adapter_down_factors[:a_width], 1, 1),
        [(i, low_all[i]) for i in range(4)],
    )
    b_p2, b_m2, b_p3, b_m3, a_total, b_total = together(
        b_p2, b_m2, b_p3, b_m3, a_total, b_total
    )
    cut = b_own.shape[0] // 2 // 16 * 16
    b_p4, b_m4 = fetch(b_p3[:cut], dz=1), fetch(b_m3[cut:], dz=-1)
    adapter_input = ((chip_sum + far_sum) * select_rows).astype(jnp.bfloat16)
    (adapter_input,) = together(adapter_input)
    up_factor_gradient = ADAPTER_SCALE * contract(adapter_input, gradients, 0, 0)
    high_all = placed(spread(high), high_m, 3)
    b_total = product(b_total, [(7, b_m2), (3, b_p2), (6, b_m3), (4, b_p3)])

    b_p4, b_m4, high_all, b_total, up_factor_gradient = together(
        b_p4, b_m4, high_all, b_total, up_factor_gradient
    )
    b_total = product(b_total, [(5, jnp.concatenate([b_p4, b_m4], 0))])
    b_out = jnp.where(active_rows[:, None], b_total, 0.0).astype(jnp.bfloat16)

    high_p, high_o, high_all, b_out, a_total = together(high_p, high_o, high_all, b_out, a_total)
    high_all = placed(placed(high_all, high_p, 1), high_o, 2)
    head_feature_gradient = in_vmem(
        last_kernel,
        head_outputs.shape,
        jnp.bfloat16,
        by_z,
        high_all.reshape(NZ // 2, by_z.shape[2], a_width),
        a_total,
        live,
        b_out,
    )
    return (head_feature_gradient, down_factor_gradient, up_factor_gradient)


def solution(mesh):
    in_specs = (
        P("dp", "tensor"),
        P(("dp", "tensor"), None),
        P("dp", "tensor"),
        P("tensor", "dp"),
        P("dp", None),
        P("dp"),
        P("dp"),
    )
    out_specs = (P("dp", "tensor"), P("tensor", "dp"), P("dp", None))
    return jax.shard_map(body, mesh=mesh, in_specs=in_specs, out_specs=out_specs, check_vma=False)
```

```python
import jax
import jax.numpy as jnp
from jax import lax
from jax.experimental import pallas as pl
from jax.experimental.pallas import tpu as pltpu
from jax.sharding import PartitionSpec as P

ADAPTER_RANK = 16
TEN_DEV = 8
ADAPTER_SCALE = 2.0
NZ, NX, NY = 8, 2, 4


def contract(left, right, left_dim, right_dim):
    return lax.dot_general(
        left, right, (((left_dim,), (right_dim,)), ((), ())), preferred_element_type=jnp.float32
    )


def fetch(x, dz=0, dx=0, dy=0):
    pairs = []
    for z in range(NZ):
        for a in range(NX):
            for y in range(NY):
                source = (((z + dz) % NZ) * NX + (a + dx) % NX) * NY + (y + dy) % NY
                pairs.append((source, (z * NX + a) * NY + y))
    return lax.ppermute(x, "dp", pairs)


def swap_tensor(x, mask):
    return lax.ppermute(x, "tensor", [(t, t ^ mask) for t in range(4)])


def together(*values):
    return lax.optimization_barrier(values)


def split_kernel(start_ref, g_ref, z_ref):
    width = z_ref.shape[2]
    for block in range(NZ):
        slot = lax.rem(block - start_ref[0] + NZ, NZ)
        z_ref[slot] = g_ref[:, block * width : (block + 1) * width]


def split_columns(gradients, start):
    rows, depth = gradients.shape
    step = rows // 4
    width = depth // NZ
    return pl.pallas_call(
        split_kernel,
        grid_spec=pltpu.PrefetchScalarGridSpec(
            num_scalar_prefetch=1,
            grid=(4,),
            in_specs=[pl.BlockSpec((step, depth), lambda i, s: (i, 0))],
            out_specs=pl.BlockSpec((NZ, step, width), lambda i, s: (0, i, 0)),
        ),
        out_shape=jax.ShapeDtypeStruct((NZ, rows, width), gradients.dtype),
        compiler_params=pltpu.CompilerParams(vmem_limit_bytes=32 * 1024 * 1024),
    )(start, gradients)


def last_kernel(z_ref, w_ref, total_ref, live_ref, b_ref, out_ref):
    width = w_ref.shape[2]
    count = w_ref.shape[0]
    total = total_ref[...]
    for i in range(count):
        total += contract(z_ref[NZ - count + i], w_ref[i], 1, 0)
    out_ref[:, :width] = jnp.where(live_ref[...] > 0, total, 0.0).astype(out_ref.dtype)
    out_ref[:, width:] = b_ref[...]


def pair_kernel(x_ref, mine_ref, far_ref, a_ref, b_ref):
    width = a_ref.shape[2]
    x = x_ref[0]
    for slot, ref in ((x, mine_ref), (1 - x, far_ref)):
        a_ref[slot] = ref[:, :width]
        b_ref[slot] = ref[:, width:]


def pairs(x, mine, far, a_width):
    rows, width = mine.shape
    shapes = [(NX, rows, a_width), (NX, rows, width - a_width)]
    vmem = pl.BlockSpec(memory_space=pltpu.VMEM)
    return pl.pallas_call(
        pair_kernel,
        in_specs=[pl.BlockSpec(memory_space=pltpu.SMEM), vmem, vmem],
        out_specs=[vmem, vmem],
        out_shape=[jax.ShapeDtypeStruct(shape, mine.dtype) for shape in shapes],
    )(x, mine, far)


def down_kernel(head_ref, back_ref, out_ref):
    out_ref[...] = ADAPTER_SCALE * contract(head_ref[...], back_ref[...], 0, 0)


def in_vmem(kernel, shape, dtype, *arrays):
    return pl.pallas_call(
        kernel,
        in_specs=[pl.BlockSpec(memory_space=pltpu.VMEM)] * len(arrays),
        out_specs=pl.BlockSpec(memory_space=pltpu.VMEM),
        out_shape=jax.ShapeDtypeStruct(shape, dtype),
        compiler_params=pltpu.CompilerParams(vmem_limit_bytes=40 * 1024 * 1024),
    )(*arrays)


def body(
    head_outputs,
    output_gradient,
    frozen_weight,
    adapter_down_factors,
    adapter_up_factors,
    tenant_index,
    tenant_group_counts,
):
    row_count = head_outputs.shape[0]
    part_rows, depth = output_gradient.shape
    shard_rows, feature_width = frozen_weight.shape
    a_width = feature_width * 5 // 8
    group = lax.axis_index("dp").astype(jnp.int32)
    z, xl, y = group // (NX * NY), (group // NY) % NX, group % NY
    tensor = lax.axis_index("tensor").astype(jnp.int32)
    zero = jnp.int32(0)

    other = fetch(frozen_weight, dx=1)
    from_core = swap_tensor(output_gradient, 1)
    partial = jnp.dot(head_outputs, adapter_down_factors, preferred_element_type=jnp.float32)
    core_partial = swap_tensor(partial, 1)
    partial, own_rows = together(partial, output_gradient)
    from_chip = swap_tensor(own_rows, 2)
    other, from_core, index_later = together(other, from_core, tenant_index)

    pair_a, pair_b = pairs(xl.reshape(1), frozen_weight, other, a_width)
    a_p1, a_m1 = fetch(pair_a, dz=1), fetch(pair_a, dz=-1)
    y_b1, y_b3 = fetch(pair_b, dy=1), fetch(pair_b, dy=-1)

    a_p1, a_m1, pair_a, pair_b, core_partial = together(a_p1, a_m1, pair_a, pair_b, core_partial)
    a_p2, a_m2 = fetch(a_p1, dz=1), fetch(a_m1, dz=-1)
    y_b = [y_b1, fetch(pair_b, dy=2), y_b3]

    def placed(array, chunk, dy):
        at = array.ndim - 3
        return lax.dynamic_update_slice_in_dim(
            array, jnp.expand_dims(chunk, at), (y + dy) % NY, at
        )

    def spread(chunk):
        at = chunk.ndim - 2
        shape = chunk.shape[:at] + (NY,) + chunk.shape[at:]
        return jnp.broadcast_to(jnp.expand_dims(chunk, at), shape)

    a_p2, a_m2 = together(a_p2, a_m2)
    low = jnp.stack([a_m1, pair_a, a_p1, a_p2])
    low_p, low_m = fetch(low, dy=1), fetch(low, dy=-1)
    a_p3, a_m3 = fetch(a_p2, dz=1), fetch(a_m2, dz=-1)
    b_own = spread(pair_b)
    for dy, chunk in zip((1, 2, 3), y_b):
        b_own = placed(b_own, chunk, dy)
    b_own = b_own.reshape(NX * NY * shard_rows, -1)

    a_p3, a_m3, b_own = together(a_p3, a_m3, b_own)
    a_p4 = fetch(a_p3, dz=1)
    b_p1, b_m1 = fetch(b_own, dz=1), fetch(b_own, dz=-1)
    high = jnp.stack([a_p3, a_p4, a_m3, a_m2])

    low_p, low_m, high, from_chip = together(low_p, low_m, high, from_chip)
    low_o, high_m = fetch(low_p, dy=1), fetch(high, dy=-1)
    b_p1, b_m1, low_p, own_rows, from_core, from_chip = together(
        b_p1, b_m1, low_p, own_rows, from_core, from_chip
    )
    b_p2, b_m2 = fetch(b_p1, dz=1), fetch(b_m1, dz=-1)

    from_both = swap_tensor(from_chip, 1)
    gradients = jnp.zeros((row_count, depth), output_gradient.dtype)
    for block, mask in ((own_rows, 0), (from_core, 1), (from_chip, 2), (from_both, 3)):
        gradients = lax.dynamic_update_slice_in_dim(
            gradients, block, (tensor ^ mask) * part_rows, 0
        )

    low_all = placed(placed(spread(low), low_p, 1), low_m, 3)

    by_z = split_columns(gradients, ((z + NZ - 1) % NZ).reshape(1))

    position = jnp.arange(row_count, dtype=jnp.int32)
    active_rows = position < tenant_group_counts[0]
    slot_lookup = jnp.arange(adapter_down_factors.shape[1], dtype=jnp.int32) // ADAPTER_RANK
    select_rows = (
        active_rows[:, None] & (slot_lookup[None, :] == (index_later % TEN_DEV)[:, None])
    ).astype(jnp.float32)
    adapter_backward = (contract(gradients, adapter_up_factors, 1, 1) * select_rows).astype(
        jnp.bfloat16
    )
    down_factor_gradient = in_vmem(
        down_kernel, adapter_down_factors.shape, jnp.float32, head_outputs, adapter_backward
    )
    live = active_rows.astype(jnp.float32)[:, None]

    def product(total, terms):
        for slot, chunk in terms:
            total = total + contract(by_z[slot], chunk.reshape(by_z.shape[2], -1), 1, 0)
        return total

    b_total = product(
        ADAPTER_SCALE * contract(adapter_backward, adapter_down_factors[a_width:], 1, 1),
        [(1, b_own), (0, b_m1), (2, b_p1)],
    )

    (
        b_p2, b_m2, low_o, high_m, high, low_all, by_z, adapter_backward, partial,
        core_partial, down_factor_gradient, b_total,
    ) = together(
        b_p2, b_m2, low_o, high_m, high, low_all, by_z, adapter_backward, partial,
        core_partial, down_factor_gradient, b_total,
    )
    high_p, high_o = fetch(high, dy=1), fetch(high_m, dy=-1)
    b_p3, b_m3 = fetch(b_p2, dz=1), fetch(b_m2, dz=-1)
    chip_sum = partial + core_partial
    far_sum = swap_tensor(chip_sum, 2)
    low_all, low_o, far_sum, chip_sum, b_q2, b_n2 = together(
        low_all, low_o, far_sum, chip_sum, b_p2, b_m2
    )
    low_all = placed(low_all, low_o, 2)
    a_total = product(
        ADAPTER_SCALE * contract(adapter_backward, adapter_down_factors[:a_width], 1, 1),
        [(i, low_all[i]) for i in range(4)],
    )
    b_p3, b_m3, a_total, chip_sum, far_sum = together(b_p3, b_m3, a_total, chip_sum, far_sum)
    cut = b_own.shape[0] // 2 // 16 * 16
    b_p4, b_m4 = fetch(b_p3[:cut], dz=1), fetch(b_m3[cut:], dz=-1)
    adapter_input = ((chip_sum + far_sum) * select_rows).astype(jnp.bfloat16)
    (adapter_input,) = together(adapter_input)
    up_factor_gradient = ADAPTER_SCALE * contract(adapter_input, gradients, 0, 0)
    high_all = placed(spread(high), high_m, 3)
    b_total = product(b_total, [(7, b_n2), (3, b_q2), (6, b_m3), (4, b_p3)])

    b_p4, b_m4, high_all, b_total, up_factor_gradient = together(
        b_p4, b_m4, high_all, b_total, up_factor_gradient
    )
    b_total = product(b_total, [(5, jnp.concatenate([b_p4, b_m4], 0))])
    b_out = jnp.where(active_rows[:, None], b_total, 0.0).astype(jnp.bfloat16)

    high_p, high_o, high_all, b_out, a_total = together(high_p, high_o, high_all, b_out, a_total)
    high_all = placed(placed(high_all, high_p, 1), high_o, 2)
    head_feature_gradient = in_vmem(
        last_kernel,
        head_outputs.shape,
        jnp.bfloat16,
        by_z,
        high_all.reshape(NZ // 2, by_z.shape[2], a_width),
        a_total,
        live,
        b_out,
    )
    return (head_feature_gradient, down_factor_gradient, up_factor_gradient)


def solution(mesh):
    in_specs = (
        P("dp", "tensor"),
        P(("dp", "tensor"), None),
        P("dp", "tensor"),
        P("tensor", "dp"),
        P("dp", None),
        P("dp"),
        P("dp"),
    )
    out_specs = (P("dp", "tensor"), P("tensor", "dp"), P("dp", None))
    return jax.shard_map(body, mesh=mesh, in_specs=in_specs, out_specs=out_specs, check_vma=False)
```

```python
import jax
import jax.numpy as jnp
from jax import lax
from jax.experimental import pallas as pl
from jax.experimental.pallas import tpu as pltpu
from jax.sharding import PartitionSpec as P

ADAPTER_RANK = 16
TEN_DEV = 8
ADAPTER_SCALE = 2.0
NZ, NX, NY = 8, 2, 4


def contract(left, right, left_dim, right_dim):
    return lax.dot_general(
        left, right, (((left_dim,), (right_dim,)), ((), ())), preferred_element_type=jnp.float32
    )


def fetch(x, dz=0, dx=0, dy=0):
    pairs = []
    for z in range(NZ):
        for a in range(NX):
            for y in range(NY):
                source = (((z + dz) % NZ) * NX + (a + dx) % NX) * NY + (y + dy) % NY
                pairs.append((source, (z * NX + a) * NY + y))
    return lax.ppermute(x, "dp", pairs)


def swap_tensor(x, mask):
    return lax.ppermute(x, "tensor", [(t, t ^ mask) for t in range(4)])


def together(*values):
    return lax.optimization_barrier(values)


def split_kernel(start_ref, g_ref, z_ref):
    width = z_ref.shape[2]
    for block in range(NZ):
        slot = lax.rem(block - start_ref[0] + NZ, NZ)
        z_ref[slot] = g_ref[:, block * width : (block + 1) * width]


def split_columns(gradients, start):
    rows, depth = gradients.shape
    step = rows // 4
    width = depth // NZ
    return pl.pallas_call(
        split_kernel,
        grid_spec=pltpu.PrefetchScalarGridSpec(
            num_scalar_prefetch=1,
            grid=(4,),
            in_specs=[pl.BlockSpec((step, depth), lambda i, s: (i, 0))],
            out_specs=pl.BlockSpec((NZ, step, width), lambda i, s: (0, i, 0)),
        ),
        out_shape=jax.ShapeDtypeStruct((NZ, rows, width), gradients.dtype),
        compiler_params=pltpu.CompilerParams(vmem_limit_bytes=32 * 1024 * 1024),
    )(start, gradients)


def last_kernel(z_ref, w_ref, total_ref, live_ref, b_ref, out_ref):
    width = w_ref.shape[2]
    count = w_ref.shape[0]
    total = total_ref[...]
    for i in range(count):
        total += contract(z_ref[NZ - count + i], w_ref[i], 1, 0)
    out_ref[:, :width] = jnp.where(live_ref[...] > 0, total, 0.0).astype(out_ref.dtype)
    out_ref[:, width:] = b_ref[...]


def pair_kernel(x_ref, mine_ref, far_ref, a_ref, b_ref):
    width = a_ref.shape[2]
    x = x_ref[0]
    for slot, ref in ((x, mine_ref), (1 - x, far_ref)):
        a_ref[slot] = ref[:, :width]
        b_ref[slot] = ref[:, width:]


def pairs(x, mine, far, a_width):
    rows, width = mine.shape
    shapes = [(NX, rows, a_width), (NX, rows, width - a_width)]
    vmem = pl.BlockSpec(memory_space=pltpu.VMEM)
    return pl.pallas_call(
        pair_kernel,
        in_specs=[pl.BlockSpec(memory_space=pltpu.SMEM), vmem, vmem],
        out_specs=[vmem, vmem],
        out_shape=[jax.ShapeDtypeStruct(shape, mine.dtype) for shape in shapes],
    )(x, mine, far)


def down_kernel(head_ref, back_ref, out_ref):
    out_ref[...] = ADAPTER_SCALE * contract(head_ref[...], back_ref[...], 0, 0)


def in_vmem(kernel, shape, dtype, *arrays):
    return pl.pallas_call(
        kernel,
        in_specs=[pl.BlockSpec(memory_space=pltpu.VMEM)] * len(arrays),
        out_specs=pl.BlockSpec(memory_space=pltpu.VMEM),
        out_shape=jax.ShapeDtypeStruct(shape, dtype),
        compiler_params=pltpu.CompilerParams(vmem_limit_bytes=40 * 1024 * 1024),
    )(*arrays)


def body(
    head_outputs,
    output_gradient,
    frozen_weight,
    adapter_down_factors,
    adapter_up_factors,
    tenant_index,
    tenant_group_counts,
):
    row_count = head_outputs.shape[0]
    part_rows, depth = output_gradient.shape
    shard_rows, feature_width = frozen_weight.shape
    a_width = feature_width * 5 // 8
    group = lax.axis_index("dp").astype(jnp.int32)
    z, xl, y = group // (NX * NY), (group // NY) % NX, group % NY
    tensor = lax.axis_index("tensor").astype(jnp.int32)
    zero = jnp.int32(0)

    other = fetch(frozen_weight, dx=1)
    from_core = swap_tensor(output_gradient, 1)
    partial = jnp.dot(head_outputs, adapter_down_factors, preferred_element_type=jnp.float32)
    core_partial = swap_tensor(partial, 1)
    partial, own_rows = together(partial, output_gradient)
    from_chip = swap_tensor(own_rows, 2)
    other, from_core, index_later = together(other, from_core, tenant_index)

    pair_a, pair_b = pairs(xl.reshape(1), frozen_weight, other, a_width)
    a_p1, a_m1 = fetch(pair_a, dz=1), fetch(pair_a, dz=-1)

    a_p1, a_m1, pair_a, pair_b, core_partial = together(a_p1, a_m1, pair_a, pair_b, core_partial)
    a_p2, a_m2 = fetch(a_p1, dz=1), fetch(a_m1, dz=-1)
    y_b = [fetch(pair_b, dy=dy) for dy in (1, 2, 3)]

    def placed(array, chunk, dy):
        at = array.ndim - 3
        return lax.dynamic_update_slice_in_dim(
            array, jnp.expand_dims(chunk, at), (y + dy) % NY, at
        )

    def spread(chunk):
        at = chunk.ndim - 2
        shape = chunk.shape[:at] + (NY,) + chunk.shape[at:]
        return jnp.broadcast_to(jnp.expand_dims(chunk, at), shape)

    a_p2, a_m2, pair_b = together(a_p2, a_m2, pair_b)
    *y_b, a_p2 = together(*y_b, a_p2)
    low = jnp.stack([a_m1, pair_a, a_p1, a_p2])
    low_p, low_m = fetch(low, dy=1), fetch(low, dy=-1)
    a_p3, a_m3 = fetch(a_p2, dz=1), fetch(a_m2, dz=-1)
    b_own = spread(pair_b)
    for dy, chunk in zip((1, 2, 3), y_b):
        b_own = placed(b_own, chunk, dy)
    b_own = b_own.reshape(NX * NY * shard_rows, -1)

    a_p3, a_m3, b_own = together(a_p3, a_m3, b_own)
    a_p4 = fetch(a_p3, dz=1)
    b_p1, b_m1 = fetch(b_own, dz=1), fetch(b_own, dz=-1)
    high = jnp.stack([a_p3, a_p4, a_m3, a_m2])

    low_p, low_m, high, from_chip = together(low_p, low_m, high, from_chip)
    low_o, high_m = fetch(low_p, dy=1), fetch(high, dy=-1)
    b_p1, b_m1, low_p, own_rows, from_core, from_chip = together(
        b_p1, b_m1, low_p, own_rows, from_core, from_chip
    )
    b_p2, b_m2 = fetch(b_p1, dz=1), fetch(b_m1, dz=-1)

    from_both = swap_tensor(from_chip, 1)
    gradients = jnp.zeros((row_count, depth), output_gradient.dtype)
    for block, mask in ((own_rows, 0), (from_core, 1), (from_chip, 2), (from_both, 3)):
        gradients = lax.dynamic_update_slice_in_dim(
            gradients, block, (tensor ^ mask) * part_rows, 0
        )

    low_all = placed(placed(spread(low), low_p, 1), low_m, 3)

    by_z = split_columns(gradients, ((z + NZ - 1) % NZ).reshape(1))

    position = jnp.arange(row_count, dtype=jnp.int32)
    active_rows = position < tenant_group_counts[0]
    slot_lookup = jnp.arange(adapter_down_factors.shape[1], dtype=jnp.int32) // ADAPTER_RANK
    select_rows = (
        active_rows[:, None] & (slot_lookup[None, :] == (index_later % TEN_DEV)[:, None])
    ).astype(jnp.float32)
    adapter_backward = (contract(gradients, adapter_up_factors, 1, 1) * select_rows).astype(
        jnp.bfloat16
    )
    down_factor_gradient = in_vmem(
        down_kernel, adapter_down_factors.shape, jnp.float32, head_outputs, adapter_backward
    )
    live = active_rows.astype(jnp.float32)[:, None]

    def product(total, terms):
        for slot, chunk in terms:
            total = total + contract(by_z[slot], chunk.reshape(by_z.shape[2], -1), 1, 0)
        return total

    b_total = product(
        ADAPTER_SCALE * contract(adapter_backward, adapter_down_factors[a_width:], 1, 1),
        [(1, b_own), (0, b_m1), (2, b_p1)],
    )

    (
        b_p2, b_m2, low_o, high_m, high, low_all, by_z, adapter_backward, partial,
        core_partial, down_factor_gradient, b_total,
    ) = together(
        b_p2, b_m2, low_o, high_m, high, low_all, by_z, adapter_backward, partial,
        core_partial, down_factor_gradient, b_total,
    )
    high_p, high_o = fetch(high, dy=1), fetch(high_m, dy=-1)
    b_p3, b_m3 = fetch(b_p2, dz=1), fetch(b_m2, dz=-1)
    chip_sum = partial + core_partial
    far_sum = swap_tensor(chip_sum, 2)
    low_all, low_o, far_sum, chip_sum, b_q2, b_n2 = together(
        low_all, low_o, far_sum, chip_sum, b_p2, b_m2
    )
    low_all = placed(low_all, low_o, 2)
    a_total = product(
        ADAPTER_SCALE * contract(adapter_backward, adapter_down_factors[:a_width], 1, 1),
        [(i, low_all[i]) for i in range(4)],
    )
    b_p3, b_m3, a_total, chip_sum, far_sum = together(b_p3, b_m3, a_total, chip_sum, far_sum)
    cut = b_own.shape[0] // 2 // 16 * 16
    b_p4, b_m4 = fetch(b_p3[:cut], dz=1), fetch(b_m3[cut:], dz=-1)
    adapter_input = ((chip_sum + far_sum) * select_rows).astype(jnp.bfloat16)
    (adapter_input,) = together(adapter_input)
    up_factor_gradient = ADAPTER_SCALE * contract(adapter_input, gradients, 0, 0)
    high_all = placed(spread(high), high_m, 3)
    b_total = product(b_total, [(7, b_n2), (3, b_q2), (6, b_m3), (4, b_p3)])

    b_p4, b_m4, high_all, b_total, up_factor_gradient = together(
        b_p4, b_m4, high_all, b_total, up_factor_gradient
    )
    b_total = product(b_total, [(5, jnp.concatenate([b_p4, b_m4], 0))])
    b_out = jnp.where(active_rows[:, None], b_total, 0.0).astype(jnp.bfloat16)

    high_p, high_o, high_all, b_out, a_total = together(high_p, high_o, high_all, b_out, a_total)
    high_all = placed(placed(high_all, high_p, 1), high_o, 2)
    head_feature_gradient = in_vmem(
        last_kernel,
        head_outputs.shape,
        jnp.bfloat16,
        by_z,
        high_all.reshape(NZ // 2, by_z.shape[2], a_width),
        a_total,
        live,
        b_out,
    )
    return (head_feature_gradient, down_factor_gradient, up_factor_gradient)


def solution(mesh):
    in_specs = (
        P("dp", "tensor"),
        P(("dp", "tensor"), None),
        P("dp", "tensor"),
        P("tensor", "dp"),
        P("dp", None),
        P("dp"),
        P("dp"),
    )
    out_specs = (P("dp", "tensor"), P("tensor", "dp"), P("dp", None))
    return jax.shard_map(body, mesh=mesh, in_specs=in_specs, out_specs=out_specs, check_vma=False)
```

```python
import jax
import jax.numpy as jnp
from jax import lax
from jax.experimental import pallas as pl
from jax.experimental.pallas import tpu as pltpu
from jax.sharding import PartitionSpec as P

ADAPTER_RANK = 16
TEN_DEV = 8
ADAPTER_SCALE = 2.0
NZ, NX, NY = 8, 2, 4


def contract(left, right, left_dim, right_dim):
    return lax.dot_general(
        left, right, (((left_dim,), (right_dim,)), ((), ())), preferred_element_type=jnp.float32
    )


def fetch(x, dz=0, dx=0, dy=0):
    pairs = []
    for z in range(NZ):
        for a in range(NX):
            for y in range(NY):
                source = (((z + dz) % NZ) * NX + (a + dx) % NX) * NY + (y + dy) % NY
                pairs.append((source, (z * NX + a) * NY + y))
    return lax.ppermute(x, "dp", pairs)


def swap_tensor(x, mask):
    return lax.ppermute(x, "tensor", [(t, t ^ mask) for t in range(4)])


def together(*values):
    return lax.optimization_barrier(values)


def split_kernel(start_ref, g_ref, z_ref):
    width = z_ref.shape[2]
    for block in range(NZ):
        slot = lax.rem(block - start_ref[0] + NZ, NZ)
        z_ref[slot] = g_ref[:, block * width : (block + 1) * width]


def split_columns(gradients, start):
    rows, depth = gradients.shape
    step = rows // 4
    width = depth // NZ
    return pl.pallas_call(
        split_kernel,
        grid_spec=pltpu.PrefetchScalarGridSpec(
            num_scalar_prefetch=1,
            grid=(4,),
            in_specs=[pl.BlockSpec((step, depth), lambda i, s: (i, 0))],
            out_specs=pl.BlockSpec((NZ, step, width), lambda i, s: (0, i, 0)),
        ),
        out_shape=jax.ShapeDtypeStruct((NZ, rows, width), gradients.dtype),
        compiler_params=pltpu.CompilerParams(vmem_limit_bytes=32 * 1024 * 1024),
    )(start, gradients)


def last_kernel(z_ref, w_ref, total_ref, live_ref, b_ref, out_ref):
    width = w_ref.shape[2]
    count = w_ref.shape[0]
    total = total_ref[...]
    for i in range(count):
        total += contract(z_ref[NZ - count + i], w_ref[i], 1, 0)
    out_ref[:, :width] = jnp.where(live_ref[...] > 0, total, 0.0).astype(out_ref.dtype)
    out_ref[:, width:] = b_ref[...]


def pair_kernel(x_ref, mine_ref, far_ref, a_ref, b_ref):
    width = a_ref.shape[2]
    x = x_ref[0]
    for slot, ref in ((x, mine_ref), (1 - x, far_ref)):
        a_ref[slot] = ref[:, :width]
        b_ref[slot] = ref[:, width:]


def pairs(x, mine, far, a_width):
    rows, width = mine.shape
    shapes = [(NX, rows, a_width), (NX, rows, width - a_width)]
    vmem = pl.BlockSpec(memory_space=pltpu.VMEM)
    return pl.pallas_call(
        pair_kernel,
        in_specs=[pl.BlockSpec(memory_space=pltpu.SMEM), vmem, vmem],
        out_specs=[vmem, vmem],
        out_shape=[jax.ShapeDtypeStruct(shape, mine.dtype) for shape in shapes],
    )(x, mine, far)


def down_kernel(head_ref, back_ref, out_ref):
    out_ref[...] = ADAPTER_SCALE * contract(head_ref[...], back_ref[...], 0, 0)


def in_vmem(kernel, shape, dtype, *arrays):
    return pl.pallas_call(
        kernel,
        in_specs=[pl.BlockSpec(memory_space=pltpu.VMEM)] * len(arrays),
        out_specs=pl.BlockSpec(memory_space=pltpu.VMEM),
        out_shape=jax.ShapeDtypeStruct(shape, dtype),
        compiler_params=pltpu.CompilerParams(vmem_limit_bytes=40 * 1024 * 1024),
    )(*arrays)


def body(
    head_outputs,
    output_gradient,
    frozen_weight,
    adapter_down_factors,
    adapter_up_factors,
    tenant_index,
    tenant_group_counts,
):
    row_count = head_outputs.shape[0]
    part_rows, depth = output_gradient.shape
    shard_rows, feature_width = frozen_weight.shape
    a_width = feature_width * 5 // 8
    group = lax.axis_index("dp").astype(jnp.int32)
    z, xl, y = group // (NX * NY), (group // NY) % NX, group % NY
    tensor = lax.axis_index("tensor").astype(jnp.int32)
    zero = jnp.int32(0)

    other = fetch(frozen_weight, dx=1)
    from_core = swap_tensor(output_gradient, 1)
    partial = jnp.dot(head_outputs, adapter_down_factors, preferred_element_type=jnp.float32)
    core_partial = swap_tensor(partial, 1)
    partial, own_rows = together(partial, output_gradient)
    from_chip = swap_tensor(own_rows, 2)
    other, from_core, index_later = together(other, from_core, tenant_index)

    pair_a, pair_b = pairs(xl.reshape(1), frozen_weight, other, a_width)
    a_p1, a_m1 = fetch(pair_a, dz=1), fetch(pair_a, dz=-1)
    y_b1, y_b3 = fetch(pair_b, dy=1), fetch(pair_b, dy=-1)

    a_p1, a_m1, pair_a, pair_b, core_partial = together(a_p1, a_m1, pair_a, pair_b, core_partial)
    a_p2, a_m2 = fetch(a_p1, dz=1), fetch(a_m1, dz=-1)
    y_b = [y_b1, fetch(pair_b, dy=2), y_b3]

    def placed(array, chunk, dy):
        at = array.ndim - 3
        return lax.dynamic_update_slice_in_dim(
            array, jnp.expand_dims(chunk, at), (y + dy) % NY, at
        )

    def spread(chunk):
        at = chunk.ndim - 2
        shape = chunk.shape[:at] + (NY,) + chunk.shape[at:]
        return jnp.broadcast_to(jnp.expand_dims(chunk, at), shape)

    a_p2, a_m2 = together(a_p2, a_m2)
    low = jnp.stack([a_m1, pair_a, a_p1, a_p2])
    low_p, low_m = fetch(low, dy=1), fetch(low, dy=-1)
    a_p3, a_m3 = fetch(a_p2, dz=1), fetch(a_m2, dz=-1)
    b_own = spread(pair_b)
    for dy, chunk in zip((1, 2, 3), y_b):
        b_own = placed(b_own, chunk, dy)
    b_own = b_own.reshape(NX * NY * shard_rows, -1)

    a_p3, a_m3, b_own = together(a_p3, a_m3, b_own)
    a_p4 = fetch(a_p3, dz=1)
    b_p1, b_m1 = fetch(b_own, dz=1), fetch(b_own, dz=-1)
    high = jnp.stack([a_p3, a_p4, a_m3, a_m2])

    low_p, low_m, high, from_chip = together(low_p, low_m, high, from_chip)
    low_o, high_m = fetch(low_p, dy=1), fetch(high, dy=-1)
    b_p1, b_m1, low_p, own_rows, from_core, from_chip = together(
        b_p1, b_m1, low_p, own_rows, from_core, from_chip
    )
    b_p2, b_m2 = fetch(b_p1, dz=1), fetch(b_m1, dz=-1)

    from_both = swap_tensor(from_chip, 1)
    partial, core_partial, from_both = together(partial, core_partial, from_both)
    chip_sum = partial + core_partial
    far_sum = swap_tensor(chip_sum, 2)
    gradients = jnp.zeros((row_count, depth), output_gradient.dtype)
    for block, mask in ((own_rows, 0), (from_core, 1), (from_chip, 2), (from_both, 3)):
        gradients = lax.dynamic_update_slice_in_dim(
            gradients, block, (tensor ^ mask) * part_rows, 0
        )

    low_all = placed(placed(spread(low), low_p, 1), low_m, 3)

    by_z = split_columns(gradients, ((z + NZ - 1) % NZ).reshape(1))

    position = jnp.arange(row_count, dtype=jnp.int32)
    active_rows = position < tenant_group_counts[0]
    slot_lookup = jnp.arange(adapter_down_factors.shape[1], dtype=jnp.int32) // ADAPTER_RANK
    select_rows = (
        active_rows[:, None] & (slot_lookup[None, :] == (index_later % TEN_DEV)[:, None])
    ).astype(jnp.float32)
    adapter_backward = (contract(gradients, adapter_up_factors, 1, 1) * select_rows).astype(
        jnp.bfloat16
    )
    down_factor_gradient = in_vmem(
        down_kernel, adapter_down_factors.shape, jnp.float32, head_outputs, adapter_backward
    )
    live = active_rows.astype(jnp.float32)[:, None]

    def product(total, terms):
        for slot, chunk in terms:
            total = total + contract(by_z[slot], chunk.reshape(by_z.shape[2], -1), 1, 0)
        return total

    b_total = product(
        ADAPTER_SCALE * contract(adapter_backward, adapter_down_factors[a_width:], 1, 1),
        [(1, b_own), (0, b_m1), (2, b_p1)],
    )

    adapter_input = ((chip_sum + far_sum) * select_rows).astype(jnp.bfloat16)
    (adapter_input,) = together(adapter_input)
    up_factor_gradient = ADAPTER_SCALE * contract(adapter_input, gradients, 0, 0)

    (
        b_p2, b_m2, low_o, high_m, high, low_all, by_z, adapter_backward,
        up_factor_gradient, down_factor_gradient, b_total,
    ) = together(
        b_p2, b_m2, low_o, high_m, high, low_all, by_z, adapter_backward,
        up_factor_gradient, down_factor_gradient, b_total,
    )
    high_p, high_o = fetch(high, dy=1), fetch(high_m, dy=-1)
    b_p3, b_m3 = fetch(b_p2, dz=1), fetch(b_m2, dz=-1)
    low_all = placed(low_all, low_o, 2)
    a_total = product(
        ADAPTER_SCALE * contract(adapter_backward, adapter_down_factors[:a_width], 1, 1),
        [(i, low_all[i]) for i in range(4)],
    )
    b_p2, b_m2, b_p3, b_m3, a_total = together(b_p2, b_m2, b_p3, b_m3, a_total)
    cut = b_own.shape[0] // 2 // 16 * 16
    b_p4, b_m4 = fetch(b_p3[:cut], dz=1), fetch(b_m3[cut:], dz=-1)
    high_all = placed(spread(high), high_m, 3)
    b_total = product(b_total, [(7, b_m2), (3, b_p2), (6, b_m3), (4, b_p3)])

    b_p4, b_m4, high_all, b_total = together(b_p4, b_m4, high_all, b_total)
    b_total = product(b_total, [(5, jnp.concatenate([b_p4, b_m4], 0))])
    b_out = jnp.where(active_rows[:, None], b_total, 0.0).astype(jnp.bfloat16)

    high_p, high_o, high_all, b_out, a_total = together(high_p, high_o, high_all, b_out, a_total)
    high_all = placed(placed(high_all, high_p, 1), high_o, 2)
    head_feature_gradient = in_vmem(
        last_kernel,
        head_outputs.shape,
        jnp.bfloat16,
        by_z,
        high_all.reshape(NZ // 2, by_z.shape[2], a_width),
        a_total,
        live,
        b_out,
    )
    return (head_feature_gradient, down_factor_gradient, up_factor_gradient)


def solution(mesh):
    in_specs = (
        P("dp", "tensor"),
        P(("dp", "tensor"), None),
        P("dp", "tensor"),
        P("tensor", "dp"),
        P("dp", None),
        P("dp"),
        P("dp"),
    )
    out_specs = (P("dp", "tensor"), P("tensor", "dp"), P("dp", None))
    return jax.shard_map(body, mesh=mesh, in_specs=in_specs, out_specs=out_specs, check_vma=False)
```
